32 devices in a mesh: dp: 4 (over y, x), fsdp: 8 (over z, core).
Axes of the slice: x: 2, y: 2, z: 4, core: 2. Of those that a mesh axis runs over, the one named last changes fastest.
Arguments:
- images: bfloat16 [128, 197, 768], P(('dp', 'fsdp')), may hold values from -6 to 6
- counts: int32 [32], P(('dp', 'fsdp')), may hold values from 1 to 4, 96 in all
- cotangent: bfloat16 [128, 197, 768], P(('dp', 'fsdp')), may hold values from -6 to 6
- w_qkv: bfloat16 [2, 768, 2304], P(None, None, ('dp', 'fsdp')), may hold values from -0.21875 to 0.21875
- w_proj: bfloat16 [2, 768, 768], P(None, None, ('dp', 'fsdp')), may hold values from -1.75 to 1.75
- w_fc1: bfloat16 [2, 768, 3072], P(None, None, ('dp', 'fsdp')), may hold values from -0.21875 to 0.21875
- w_fc2: bfloat16 [2, 3072, 768], P(None, None, ('dp', 'fsdp')), may hold values from -0.109375 to 0.109375
- gains: bfloat16 [2, 2, 768], P(None, None, ('dp', 'fsdp')), may hold values from 0.25 to 1.75
- biases: bfloat16 [2, 6, 768], P(None, None, ('dp', 'fsdp')), may hold values from -1.5 to 1.5
- fc1_bias: bfloat16 [2, 1, 3072], P(None, None, ('dp', 'fsdp')), may hold values from -1.5 to 1.5
Outputs:
- block_output: bfloat16 [128, 197, 768], P(('dp', 'fsdp'))
- grad_images: float32 [128, 197, 768], P(('dp', 'fsdp'))
- grad_w_qkv: float32 [2, 768, 2304], P(None, None, ('dp', 'fsdp'))
- grad_w_proj: float32 [2, 768, 768], P(None, None, ('dp', 'fsdp'))
- grad_w_fc1: float32 [2, 768, 3072], P(None, None, ('dp', 'fsdp'))
- grad_w_fc2: float32 [2, 3072, 768], P(None, None, ('dp', 'fsdp'))
- grad_gains: float32 [2, 2, 768], P(None, None, ('dp', 'fsdp'))
- grad_biases: float32 [2, 6, 768], P(None, None, ('dp', 'fsdp'))
- grad_fc1_bias: float32 [2, 1, 3072], P(None, None, ('dp', 'fsdp'))
The draws below stay inside these ranges and needn't reach their ends.
Inputs may be any that keep to these rules, and one draw needn't show every extreme that they name: counts[i] is how many of device i's 4 image slots hold live images, which come first; the counts add up to 96 and the largest is 4.
All inputs are finite; a program needn't handle non-finite values.
Results may differ from the reference program's by a relative error of at most 0.013.
Values may be sent and summed in bfloat16 or wider, within the bound.
No kernel may reach another device: no remote copies, remote signals or barrier semaphores. Data moves between devices by JAX's collectives and lax.ppermute only.
A program may use at most 256 MiB of HBM per device.

```python
import math
import jax
import jax.numpy as jnp
import numpy as np
from jax import lax

D = 768
HEADS = 12
HEAD_DIM = 64
FF = 3072
SEQ = 197
LAYERS = 2
CAP = 4
IMAGES = 128
LIVE_IMAGES = 96
DEVICES = 32


def strengthened(drawn, key, source, target, shards_of, factor):
    def block_of(position):
        return (jnp.arange(drawn.shape[position]) // (drawn.shape[position] // shards_of)).reshape((-1,) + (1,) * (drawn.ndim - 1 - position))

    near = jax.random.permutation(key, shards_of)[block_of(target)]
    other_side = (block_of(target) + shards_of // 2) % shards_of
    return jnp.where((block_of(source) == near) | (block_of(source) == other_side), factor * drawn, drawn)


def shard_levels(rng, shape, cuts, low, largest):
    def one(dim, parts):
        heights = jax.random.uniform(jax.random.fold_in(jax.random.fold_in(rng, 6), dim), (parts,), jnp.float32, low / len(cuts), largest / len(cuts))
        return jnp.repeat(jnp.exp(heights), shape[dim] // parts).reshape((-1,) + (1,) * (len(shape) - dim - 1))

    gain = one(*cuts[0])
    for cut in cuts[1:]:
        gain = gain * one(*cut)
    return gain


def length_profile(count, total, limit, lean):
    portions = [(1 << 20) // math.isqrt(standing ** lean) + 1 for standing in range(2, count + 1)]
    surplus, given = total - limit - (count - 1), [1] * (count - 1)
    while surplus > 0:
        free = [i for i in range(count - 1) if given[i] < limit]
        pool, left = sum([portions[i] for i in free]), surplus
        for i in free:
            addition = min(limit - given[i], max(1, left * portions[i] // pool), surplus)
            given[i] = given[i] + addition
            surplus = surplus - addition
    return np.array([limit] + given)


def ragged_sizes(own_key, count, total, limit, slope):
    if count == 2:
        one = jax.random.randint(own_key, (), max(1, total - limit), min(limit, total - 1) + 1)
        return jnp.stack([one, total - one])
    tallies = jnp.asarray(length_profile(count, total, limit, slope), jnp.int32)
    pairs = (count - 1) // 2
    giver, receiver = tallies[1:1 + 2 * pairs:2], tallies[2:2 + 2 * pairs:2]
    margin = jnp.minimum(giver - 1, limit - receiver)
    passed = jax.random.randint(jax.random.fold_in(own_key, 1), (pairs,), 0, 1 << 20) % (margin + 1)
    tallies = tallies.at[1:1 + 2 * pairs:2].set(giver - passed).at[2:2 + 2 * pairs:2].set(receiver + passed)
    return tallies[jax.random.permutation(jax.random.fold_in(own_key, 2), count)]


def centred(stream_key, dims, width, most, pieces=(), held_as=jnp.bfloat16):
    values = jax.random.normal(stream_key, dims, jnp.float32) * width
    if len(pieces) > 0:
        values = shard_levels(stream_key, dims, pieces, -0.22, 0.18) * values
    return jnp.clip(values, min=-most, max=most).astype(held_as)


def heavy_noise(stream_key, extent, deviation, limit, cuts, heavy, dtype=jnp.bfloat16):
    drawn = deviation * jax.random.normal(stream_key, extent, jnp.float32)
    if cuts:
        drawn = drawn * shard_levels(stream_key, extent, cuts, -0.22, 0.18)
    return jnp.clip(strengthened(drawn, jax.random.fold_in(stream_key, 3), *heavy), -limit, limit).astype(dtype)


def setup_inputs(seed: int = 0) -> dict:
    splits = jax.random.split(jax.random.key(seed), 11)
    images = centred(splits[0], (IMAGES, SEQ, D), 1.0, 6.0, ((0, 32),))
    counts = ragged_sizes(splits[1], DEVICES, LIVE_IMAGES, CAP, 2).astype(jnp.int32)
    cotangent = heavy_noise(splits[2], (IMAGES, SEQ, D), 1.0, 6.0, ((0, 32),), (0, 2, 32, 2.75))
    w_qkv = centred(splits[3], (LAYERS, D, 3 * D), D ** -0.5, 0.21875, ((2, 32),))
    w_proj = centred(splits[4], (LAYERS, D, D), (D // 64) ** -0.5, 1.75, ((2, 32),))
    w_fc1 = centred(splits[5], (LAYERS, D, FF), D ** -0.5, 0.21875, ((2, 32),))
    w_fc2 = centred(splits[6], (LAYERS, FF, D), FF ** -0.5, 0.109375, ((2, 32),))
    gains = jnp.clip(1.0 + 0.15 * jax.random.normal(splits[7], (LAYERS, 2, D), jnp.float32), 0.25, 1.75).astype(jnp.bfloat16)
    biases = centred(splits[8], (LAYERS, 6, D), 0.3, 1.5, ((2, 32),))
    fc1_bias = centred(splits[9], (LAYERS, 1, FF), 0.3, 1.5, ((2, 32),))
    return {"images": images, "counts": counts, "cotangent": cotangent, "w_qkv": w_qkv, "w_proj": w_proj, "w_fc1": w_fc1, "w_fc2": w_fc2, "gains": gains, "biases": biases, "fc1_bias": fc1_bias}


@jax.custom_vjp
def low(v):
    return lax.optimization_barrier(v.astype(jnp.bfloat16)).astype(jnp.float32)

@jax.custom_vjp
def low_back(v):
    return v

def low_keep(v):
    return (low(v), None)

def low_pass(kept, grad):
    return (grad,)

def back_keep(v):
    return (v, None)

def back_low(kept, grad):
    return (low(grad),)
low.defvjp(low_keep, low_pass)
low_back.defvjp(back_keep, back_low)

def both_round(value):
    return low_back(low(value))

def layer_norm(token_rows, gain_row, shift_row):
    row_mean = lax.optimization_barrier(jnp.mean(token_rows, -1, keepdims=True))
    centered = token_rows - row_mean
    row_var = lax.optimization_barrier(jnp.mean(centered * centered, -1, keepdims=True))
    return centered * lax.rsqrt(row_var + 1e-06) * gain_row + shift_row

def matmul(left, right):
    return jnp.dot(left, right, precision=lax.Precision.HIGHEST)

def one_layer(state, w_qkv, w_proj, w_fc1, w_fc2, gains, biases, fc1_bias):
    token_rows = state.reshape(-1, D)
    normed_one = low(layer_norm(token_rows, gains[0], biases[0]))
    mixed = matmul(normed_one, w_qkv)
    head_shape = (state.shape[0], SEQ, HEADS, HEAD_DIM)
    query_heads = both_round(mixed[:, :D] + biases[1]).reshape(head_shape)
    key_heads = both_round(mixed[:, D:2 * D]).reshape(head_shape)
    value_heads = both_round(mixed[:, 2 * D:] + biases[2]).reshape(head_shape)
    scores = jnp.einsum('bqhd,bkhd->bhqk', query_heads, key_heads, precision=lax.Precision.HIGHEST)
    scores = low_back(scores * HEAD_DIM ** (-0.5))
    attn_probs = low(jax.nn.softmax(scores, axis=-1))
    attended = jnp.einsum('bhqk,bkhd->bqhd', attn_probs, value_heads, precision=lax.Precision.HIGHEST)
    attended = both_round(attended.reshape(-1, D))
    middle = token_rows + low_back(matmul(attended, w_proj) + biases[3])
    normed_two = low(layer_norm(middle, gains[1], biases[4]))
    hidden_pre = low_back(matmul(normed_two, w_fc1) + fc1_bias[0])
    hidden = low(jax.nn.gelu(hidden_pre, approximate=False))
    final = middle + low_back(matmul(hidden, w_fc2) + biases[5])
    return final.reshape(state.shape)

def reference(images, counts, cotangent, w_qkv, w_proj, w_fc1, w_fc2, gains, biases, fc1_bias):
    live = (jnp.arange(IMAGES) % CAP < jnp.repeat(counts, CAP)).astype(jnp.float32)[:, None, None]

    def forward(image_rows, wq, wp, wa, wb, gain_all, bias_all, fc1_all):

        def per_group(carry, group):
            state = group
            for layer_index in range(LAYERS):
                state = one_layer(state, wq[layer_index], wp[layer_index], wa[layer_index], wb[layer_index], gain_all[layer_index], bias_all[layer_index], fc1_all[layer_index])
            return (carry, state)
        grouped = image_rows.reshape(IMAGES // CAP, CAP, SEQ, D)
        unused, result = lax.scan(jax.checkpoint(per_group), jnp.zeros((), jnp.float32), grouped)
        return result.reshape(IMAGES, SEQ, D) * live
    primals = tuple((item.astype(jnp.float32) for item in (images, w_qkv, w_proj, w_fc1, w_fc2, gains, biases, fc1_bias)))
    output, pullback = jax.vjp(forward, *primals)
    grads = pullback(cotangent.astype(jnp.float32))
    return (output.astype(jnp.bfloat16), grads[0], grads[1], grads[2], grads[3], grads[4], grads[5], grads[6], grads[7])
```

```python
from functools import partial

import jax
import jax.numpy as jnp
from jax import lax
from jax.sharding import PartitionSpec as P

HEAD_DIM = 64


def inner_rows(left, right):
    return lax.dot_general(
        left, right, (((0,), (0,)), ((), ())), preferred_element_type=jnp.float32
    )


def times_transposed(left, right):
    return lax.dot_general(
        left, right, (((1,), (1,)), ((), ())), preferred_element_type=jnp.float32
    )


def norm_parts(token_rows):
    row_mean = jnp.mean(token_rows, -1, keepdims=True)
    centered = token_rows - row_mean
    inv_std = lax.rsqrt(jnp.mean(centered * centered, -1, keepdims=True) + 1e-06)
    return (centered * inv_std, inv_std)


def norm_back(grad_normed, scaled, inv_std, gain_row):
    grad_scaled = grad_normed * gain_row
    return inv_std * (
        grad_scaled
        - jnp.mean(grad_scaled, -1, keepdims=True)
        - scaled * jnp.mean(grad_scaled * scaled, -1, keepdims=True)
    )


def layer_forward(state, full_weights, heads):
    w_qkv, w_proj, w_fc1, w_fc2, gains, biases, fc1_bias = full_weights
    gains = gains.astype(jnp.float32)
    biases = biases.astype(jnp.float32)
    slots, seq_len, width = state.shape
    head_shape = (slots, seq_len, heads, width // heads)
    token_rows = state.reshape(-1, width)
    scaled_one, inv_one = norm_parts(token_rows)
    normed_one = (scaled_one * gains[0] + biases[0]).astype(jnp.bfloat16)
    mixed = times_transposed(normed_one, w_qkv)
    query_heads = (mixed[:, :width] + biases[1]).astype(jnp.bfloat16).reshape(head_shape)
    key_heads = mixed[:, width : 2 * width].astype(jnp.bfloat16).reshape(head_shape)
    value_heads = (mixed[:, 2 * width :] + biases[2]).astype(jnp.bfloat16).reshape(head_shape)
    scores = jnp.einsum(
        "bqhd,bkhd->bhqk", query_heads, key_heads, preferred_element_type=jnp.float32
    )
    scores = scores * HEAD_DIM ** (-0.5)
    top_score = jnp.max(scores, -1, keepdims=True)
    expo_score = jnp.exp(scores - top_score)
    total_score = jnp.sum(expo_score, -1, keepdims=True)
    attn_probs = (expo_score / total_score).astype(jnp.bfloat16)
    log_total = top_score + jnp.log(total_score)
    attended = jnp.einsum(
        "bhqk,bkhd->bqhd", attn_probs, value_heads, preferred_element_type=jnp.float32
    )
    attended = attended.reshape(-1, width).astype(jnp.bfloat16)
    middle = token_rows + times_transposed(attended, w_proj) + biases[3]
    scaled_two, inv_two = norm_parts(middle)
    normed_two = (scaled_two * gains[1] + biases[4]).astype(jnp.bfloat16)
    hidden_pre = times_transposed(normed_two, w_fc1) + fc1_bias[
        0
    ].astype(jnp.float32)
    hidden = jax.nn.gelu(hidden_pre, approximate=False).astype(jnp.bfloat16)
    final = middle + times_transposed(hidden, w_fc2) + biases[5]
    kept = (
        token_rows,
        query_heads,
        key_heads,
        value_heads,
        log_total,
        attended,
        middle,
        hidden_pre,
    )
    return (final.reshape(state.shape), kept)


def layer_backward(grad_final, kept, full_weights):
    w_qkv, w_proj, w_fc1, w_fc2, gains, biases, fc1_bias = full_weights
    gains = gains.astype(jnp.float32)
    biases = biases.astype(jnp.float32)
    token_rows, query_heads, key_heads, value_heads, log_total, attended, middle, hidden_pre = kept
    width = token_rows.shape[1]
    scaled_one, inv_one = norm_parts(token_rows)
    normed_one = (scaled_one * gains[0] + biases[0]).astype(jnp.bfloat16)
    scaled_two, inv_two = norm_parts(middle)
    normed_two = (scaled_two * gains[1] + biases[4]).astype(jnp.bfloat16)
    gelu_value, gelu_pull = jax.vjp(partial(jax.nn.gelu, approximate=False), hidden_pre)
    hidden = gelu_value.astype(jnp.bfloat16)
    branch_two = grad_final.astype(jnp.bfloat16)
    grad_fc2 = inner_rows(branch_two, hidden)
    grad_fc2_bias = jnp.sum(branch_two.astype(jnp.float32), 0)
    grad_hidden = jnp.dot(branch_two, w_fc2, preferred_element_type=jnp.float32)
    grad_pre = gelu_pull(grad_hidden)[0].astype(jnp.bfloat16)
    grad_fc1 = inner_rows(grad_pre, normed_two)
    grad_fc1_bias = jnp.sum(grad_pre.astype(jnp.float32), 0)
    grad_normed_two = jnp.dot(grad_pre, w_fc1, preferred_element_type=jnp.float32)
    grad_gain_two = jnp.sum(grad_normed_two * scaled_two, 0)
    grad_shift_two = jnp.sum(grad_normed_two, 0)
    grad_middle = grad_final + norm_back(grad_normed_two, scaled_two, inv_two, gains[1])
    branch_one = grad_middle.astype(jnp.bfloat16)
    grad_proj = inner_rows(branch_one, attended)
    grad_proj_bias = jnp.sum(branch_one.astype(jnp.float32), 0)
    grad_attended = (
        jnp.dot(branch_one, w_proj, preferred_element_type=jnp.float32).astype(jnp.bfloat16).reshape(query_heads.shape)
    )
    scores = jnp.einsum(
        "bqhd,bkhd->bhqk", query_heads, key_heads, preferred_element_type=jnp.float32
    )
    scores = scores * HEAD_DIM ** (-0.5)
    attn_exact = jnp.exp(scores - log_total)
    attn_probs = attn_exact.astype(jnp.bfloat16)
    grad_values = jnp.einsum(
        "bhqk,bqhd->bkhd", attn_probs, grad_attended, preferred_element_type=jnp.float32
    )
    grad_probs = jnp.einsum(
        "bqhd,bkhd->bhqk", grad_attended, value_heads, preferred_element_type=jnp.float32
    )
    row_inner = jnp.sum(grad_probs * attn_exact, -1, keepdims=True)
    grad_scores = (attn_exact * (grad_probs - row_inner)).astype(jnp.bfloat16)
    grad_query = jnp.einsum(
        "bhqk,bkhd->bqhd", grad_scores, key_heads, preferred_element_type=jnp.float32
    )
    grad_keys = jnp.einsum(
        "bhqk,bqhd->bkhd", grad_scores, query_heads, preferred_element_type=jnp.float32
    )
    grad_mixed = jnp.concatenate(
        [
            (grad_query * HEAD_DIM ** (-0.5)).reshape(-1, width),
            (grad_keys * HEAD_DIM ** (-0.5)).reshape(-1, width),
            grad_values.reshape(-1, width),
        ],
        1,
    ).astype(jnp.bfloat16)
    grad_qkv = inner_rows(grad_mixed, normed_one)
    grad_columns = jnp.sum(grad_mixed.astype(jnp.float32), 0)
    grad_normed_one = jnp.dot(grad_mixed, w_qkv, preferred_element_type=jnp.float32)
    grad_gain_one = jnp.sum(grad_normed_one * scaled_one, 0)
    grad_shift_one = jnp.sum(grad_normed_one, 0)
    grad_input = grad_middle + norm_back(grad_normed_one, scaled_one, inv_one, gains[0])
    gains_grad = jnp.stack([grad_gain_one, grad_gain_two])
    biases_grad = jnp.stack(
        [
            grad_shift_one,
            grad_columns[:width],
            grad_columns[2 * width :],
            grad_proj_bias,
            grad_shift_two,
            grad_fc2_bias,
        ]
    )
    grads = (grad_qkv, grad_proj, grad_fc1, grad_fc2, gains_grad, biases_grad, grad_fc1_bias[None])
    return (grad_input, grads)


AXES = ("dp", "fsdp")


def pack_layer(w_qkv, w_proj, w_fc1, w_fc2, gains, biases, fc1_bias):
    width, tall = w_qkv.shape[0], w_fc2.shape[0]
    cut = w_fc2.T.reshape(w_fc2.shape[1], tall // width, width).transpose(1, 0, 2)
    small = jnp.concatenate([gains.reshape(-1), biases.reshape(-1), fc1_bias.reshape(-1)])
    small = jnp.pad(small, (0, -small.size % width)).reshape(-1, width)
    small = jnp.pad(small, ((0, -small.shape[0] % 16), (0, 0)))
    return jnp.concatenate([w_qkv.T, w_proj.T, w_fc1.T, cut.reshape(-1, width), small], 0)


def unpack_layer(blob, shapes):
    devices, _, width = blob.shape
    qkv, proj, fc1, fc2, gains, biases, fc1_bias = shapes
    at = 0
    parts = []
    for columns in (qkv[1], proj[1], fc1[1]):
        parts.append(blob[:, at : at + columns].reshape(-1, width))
        at += columns
    blocks = fc2[0] // width
    cut = blob[:, at : at + blocks * fc2[1]].reshape(devices, blocks, fc2[1], width)
    parts.append(cut.transpose(0, 2, 1, 3).reshape(devices * fc2[1], fc2[0]))
    at += blocks * fc2[1]
    small = blob[:, at:].reshape(devices, -1)
    start = 0
    for rows, columns in (gains, biases, fc1_bias):
        piece = small[:, start : start + rows * columns].reshape(devices, rows, columns)
        parts.append(piece.transpose(1, 0, 2).reshape(rows, devices * columns))
        start += rows * columns
    return tuple(parts)


def pack_grads(grads, shapes, total_rows, devices):
    grad_qkv, grad_proj, grad_fc1, grad_fc2, gains_grad, biases_grad, fc1_grad = grads
    width = grad_qkv.shape[1]
    qkv, proj, fc1, fc2, gains, biases, fc1_bias = shapes
    blob = jnp.zeros((devices, total_rows, width), jnp.bfloat16)
    at = 0
    for value in (grad_qkv, grad_proj, grad_fc1):
        rows = value.shape[0] // devices
        blob = blob.at[:, at : at + rows].set(
            value.astype(jnp.bfloat16).reshape(devices, rows, width)
        )
        at += rows
    blocks = fc2[0] // width
    cut = grad_fc2.astype(jnp.bfloat16).reshape(devices, fc2[1], blocks, width).transpose(0, 2, 1, 3)
    blob = blob.at[:, at : at + blocks * fc2[1]].set(cut.reshape(devices, -1, width))
    at += blocks * fc2[1]
    small = []
    for value, (rows, columns) in ((gains_grad, gains), (biases_grad, biases), (fc1_grad, fc1_bias)):
        small.append(value.reshape(rows, devices, columns).transpose(1, 0, 2).reshape(devices, -1))
    small = jnp.concatenate(small, 1).astype(jnp.bfloat16)
    small = jnp.pad(small, ((0, 0), (0, -small.shape[1] % width))).reshape(devices, -1, width)
    return blob.at[:, at : at + small.shape[1]].set(small)


def unpack_grads(blob, shapes):
    width = blob.shape[1]
    qkv, proj, fc1, fc2, gains, biases, fc1_bias = shapes
    blob = blob.astype(jnp.float32)
    at = 0
    parts = []
    for columns in (qkv[1], proj[1], fc1[1]):
        parts.append(blob[at : at + columns].T)
        at += columns
    blocks = fc2[0] // width
    cut = blob[at : at + blocks * fc2[1]].reshape(blocks, fc2[1], width)
    parts.append(cut.transpose(0, 2, 1).reshape(fc2))
    at += blocks * fc2[1]
    small = blob[at:].reshape(-1)
    start = 0
    for rows, columns in (gains, biases, fc1_bias):
        parts.append(small[start : start + rows * columns].reshape(rows, columns))
        start += rows * columns
    return tuple(parts)


def on_device(images, counts, cotangent, *weights):
    slots, seq_len, width = images.shape
    heads = width // HEAD_DIM
    layer_count = weights[0].shape[0]
    shapes = [w.shape[1:] for w in weights]
    live = (jnp.arange(slots) < counts[0]).astype(jnp.float32)[:, None, None]
    state = images.astype(jnp.float32)
    kept_layers = []
    gathered_layers = []
    for layer_index in range(layer_count):
        share = pack_layer(*(w[layer_index] for w in weights))
        blob = lax.all_gather(share, AXES, axis=0, tiled=False)
        gathered_layers.append(unpack_layer(blob, shapes))
    for layer_index in range(layer_count):
        state, kept = layer_forward(state, gathered_layers[layer_index], heads)
        kept_layers.append(kept)
    block_output = (state * live).astype(jnp.bfloat16)
    grad_state = (cotangent.astype(jnp.float32) * live).reshape(-1, width)
    layer_grads = [None] * layer_count
    for layer_index in reversed(range(layer_count)):
        grad_state, grads = layer_backward(
            grad_state, kept_layers[layer_index], gathered_layers[layer_index]
        )
        packed = pack_grads(grads, shapes, share.shape[0], blob.shape[0])
        summed = lax.psum_scatter(packed, AXES, scatter_dimension=0, tiled=False)
        layer_grads[layer_index] = unpack_grads(summed, shapes)
    stacked = tuple((jnp.stack([entry[member] for entry in layer_grads]) for member in range(7)))
    return (block_output, grad_state.reshape(images.shape), *stacked)


def solution(mesh):
    placed = (
        P(("dp", "fsdp"), None, None),
        P(("dp", "fsdp")),
        P(("dp", "fsdp"), None, None),
        P(None, None, ("dp", "fsdp")),
        P(None, None, ("dp", "fsdp")),
        P(None, None, ("dp", "fsdp")),
        P(None, None, ("dp", "fsdp")),
        P(None, None, ("dp", "fsdp")),
        P(None, None, ("dp", "fsdp")),
        P(None, None, ("dp", "fsdp")),
    )
    return jax.shard_map(
        on_device,
        mesh=mesh,
        in_specs=placed,
        out_specs=(
            P(("dp", "fsdp"), None, None),
            P(("dp", "fsdp"), None, None),
            P(None, None, ("dp", "fsdp")),
            P(None, None, ("dp", "fsdp")),
            P(None, None, ("dp", "fsdp")),
            P(None, None, ("dp", "fsdp")),
            P(None, None, ("dp", "fsdp")),
            P(None, None, ("dp", "fsdp")),
            P(None, None, ("dp", "fsdp")),
        ),
        check_vma=False,
    )
```

```python
import math
from functools import partial

import jax
import jax.numpy as jnp
from jax import lax
from jax.experimental import pallas as pl
from jax.experimental.pallas import tpu as pltpu
from jax.sharding import PartitionSpec as P

HEAD_DIM = 64
MATMUL_NT = (((1,), (1,)), ((), ()))
MATMUL_NN = (((1,), (0,)), ((), ()))
MATMUL_TN = (((0,), (0,)), ((), ()))
VMEM_BYTES = 60 * 1024 * 1024
TILE_ROWS = 16
LANES = 128
MASKED = -1e30


def dot(left, right, dims):
    return lax.dot_general(left, right, dims, preferred_element_type=jnp.float32)


def norm_parts(token_rows):
    row_mean = jnp.mean(token_rows, -1, keepdims=True)
    centered = token_rows - row_mean
    inv_std = lax.rsqrt(jnp.mean(centered * centered, -1, keepdims=True) + 1e-06)
    return (centered * inv_std, inv_std)


def norm_back(grad_normed, scaled, inv_std, gain_row):
    grad_scaled = grad_normed * gain_row
    return inv_std * (
        grad_scaled
        - jnp.mean(grad_scaled, -1, keepdims=True)
        - scaled * jnp.mean(grad_scaled * scaled, -1, keepdims=True)
    )


def column_sums(rows):
    return jnp.sum(rows.astype(jnp.float32), 0, keepdims=True)


def side_of(pair, side):
    lane = lax.broadcasted_iota(jnp.int32, pair.shape, 1)
    mine = (lane >= HEAD_DIM) if side else (lane < HEAD_DIM)
    return jnp.where(mine, pair, jnp.zeros_like(pair))


def attn_forward_kernel(seq_len, x_ref, w_qkv_ref, w_proj_ref, gains_ref, biases_ref,
                        normed_ref, mixed_ref, probs_ref, attended_ref, middle_ref):
    width = x_ref.shape[2]
    token_rows = x_ref[0]
    scaled, _ = norm_parts(token_rows)
    normed = (scaled * gains_ref[0:1] + biases_ref[0:1]).astype(jnp.bfloat16)
    normed_ref[0] = normed
    for part in range(3):
        columns = slice(part * width, (part + 1) * width)
        mixed = dot(normed, w_qkv_ref[columns, :], MATMUL_NT)
        if part == 0:
            mixed = mixed + biases_ref[1:2]
        if part == 2:
            mixed = mixed + biases_ref[2:3]
        mixed = mixed.astype(jnp.bfloat16)
        if part == 0:
            mixed = mixed * jnp.bfloat16(HEAD_DIM ** (-0.5))
        mixed_ref[0, :, columns] = mixed
    padded = x_ref.shape[1]
    real_key = lax.broadcasted_iota(jnp.int32, (padded, padded), 1) < seq_len
    for pair in range(width // LANES):
        at = pair * LANES
        query = mixed_ref[0, :, at : at + LANES]
        key = mixed_ref[0, :, width + at : width + at + LANES]
        value = mixed_ref[0, :, 2 * width + at : 2 * width + at + LANES]
        total = None
        for side in range(2):
            scores = dot(side_of(query, side), key, MATMUL_NT)
            scores = jnp.where(real_key, scores, MASKED)
            top = jnp.max(scores, -1, keepdims=True)
            expo = jnp.exp(scores - top)
            probs = (expo / jnp.sum(expo, -1, keepdims=True)).astype(jnp.bfloat16)
            probs_ref[0, 2 * pair + side] = probs
            part = dot(probs, side_of(value, side), MATMUL_NN)
            total = part if total is None else total + part
        attended_ref[0, :, at : at + LANES] = total.astype(jnp.bfloat16)
    middle_ref[0] = (
        token_rows + dot(attended_ref[0], w_proj_ref[...], MATMUL_NT) + biases_ref[3:4]
    )


def whole(shape):
    return pl.BlockSpec(shape, lambda i: (0,) * len(shape))


def slot_block(shape):
    return pl.BlockSpec((1, *shape[1:]), lambda i: (i,) + (0,) * (len(shape) - 1))


def worth(microseconds):
    return pl.CostEstimate(
        flops=int(microseconds * 1e9), bytes_accessed=1 << 20, transcendentals=0
    )


def params():
    return pltpu.CompilerParams(
        dimension_semantics=("arbitrary",), vmem_limit_bytes=VMEM_BYTES
    )


def attn_forward(state, w_qkv, w_proj, gains, biases, seq_len):
    slots, padded, width = state.shape
    heads = width // HEAD_DIM
    outs = [
        jax.ShapeDtypeStruct((slots, padded, width), jnp.bfloat16),
        jax.ShapeDtypeStruct((slots, padded, 3 * width), jnp.bfloat16),
        jax.ShapeDtypeStruct((slots, heads, padded, padded), jnp.bfloat16),
        jax.ShapeDtypeStruct((slots, padded, width), jnp.bfloat16),
        jax.ShapeDtypeStruct((slots, padded, width), jnp.float32),
    ]
    return pl.pallas_call(
        partial(attn_forward_kernel, seq_len),
        grid=(slots,),
        in_specs=[slot_block(state.shape)]
        + [whole(v.shape) for v in (w_qkv, w_proj, gains, biases)],
        out_specs=[slot_block(o.shape) for o in outs],
        out_shape=outs,
        compiler_params=params(),
        cost_estimate=worth(18),
        name="attn_forward",
    )(state, w_qkv, w_proj, gains, biases)


def mlp_forward_kernel(middle_ref, w_fc1_ref, w_fc2_ref, gains_ref, biases_ref, fc1_bias_ref,
                       normed_ref, hidden_ref, slope_ref, final_ref):
    block = pl.program_id(0)
    slots = middle_ref.shape[0]

    @pl.when(block == 0)
    def _():
        def first(slot, carry):
            middle = middle_ref[slot]
            scaled, _ = norm_parts(middle)
            normed_ref[slot] = (scaled * gains_ref[1:2] + biases_ref[4:5]).astype(jnp.bfloat16)
            final_ref[slot] = middle + biases_ref[5:6]
            return carry

        lax.fori_loop(0, slots, first, 0)

    def rows(slot, carry):
        pre = dot(normed_ref[slot], w_fc1_ref[...], MATMUL_NT) + fc1_bias_ref[0]
        below = 0.5 * (1.0 + lax.erf(pre * 0.5**0.5))
        hidden = (pre * below).astype(jnp.bfloat16)
        bell = jnp.exp(-0.5 * (pre * pre)) * (2.0 * math.pi) ** -0.5
        slope_ref[slot] = (below + pre * bell).astype(jnp.bfloat16)
        hidden_ref[slot] = hidden
        final_ref[slot] += dot(hidden, w_fc2_ref[0], MATMUL_NT)
        return carry

    lax.fori_loop(0, slots, rows, 0)


def mlp_forward(middle, w_fc1, w_fc2, gains, biases, fc1_bias):
    slots, padded, width = middle.shape
    blocks = w_fc2.shape[0]
    wide = (slots, padded, blocks * width)
    outs = [
        jax.ShapeDtypeStruct(middle.shape, jnp.bfloat16),
        jax.ShapeDtypeStruct(wide, jnp.bfloat16),
        jax.ShapeDtypeStruct(wide, jnp.bfloat16),
        jax.ShapeDtypeStruct(middle.shape, jnp.float32),
    ]
    wide_spec = pl.BlockSpec((slots, padded, width), lambda i: (0, 0, i))
    return pl.pallas_call(
        mlp_forward_kernel,
        grid=(blocks,),
        in_specs=[
            whole(middle.shape),
            pl.BlockSpec((width, width), lambda i: (i, 0)),
            pl.BlockSpec((1, width, width), lambda i: (i, 0, 0)),
            whole(gains.shape),
            whole(biases.shape),
            pl.BlockSpec((1, 1, width), lambda i: (i, 0, 0)),
        ],
        out_specs=[whole(middle.shape), wide_spec, wide_spec, whole(middle.shape)],
        out_shape=outs,
        compiler_params=params(),
        cost_estimate=worth(24),
        name="mlp_forward",
    )(middle, w_fc1, w_fc2, gains, biases, fc1_bias)


def mlp_backward_kernel(grad_ref, middle_ref, normed_ref, hidden_ref, slope_ref, w_fc1_ref,
                        w_fc2_ref, gains_ref,
                        grad_fc1_ref, grad_fc2_ref, fc1_sums_ref, sums_ref, out_ref,
                        branch_ref, pre_ref, total_ref):
    block = pl.program_id(0)
    slots, padded, width = grad_ref.shape

    @pl.when(block == 0)
    def _():
        sums_ref[...] = jnp.zeros_like(sums_ref)

        def first(slot, carry):
            branch = grad_ref[slot].astype(jnp.bfloat16)
            branch_ref[pl.ds(pl.multiple_of(slot * padded, TILE_ROWS), padded), :] = branch
            sums_ref[2:3] += column_sums(branch)
            return carry

        lax.fori_loop(0, slots, first, 0)

    fc1_sums_ref[...] = jnp.zeros_like(fc1_sums_ref)

    def rows(slot, carry):
        here = pl.ds(pl.multiple_of(slot * padded, TILE_ROWS), padded)
        grad_hidden = dot(branch_ref[here, :], w_fc2_ref[0], MATMUL_NN)
        grad_pre = (grad_hidden * slope_ref[slot].astype(jnp.float32)).astype(jnp.bfloat16)
        pre_ref[here, :] = grad_pre
        fc1_sums_ref[0, 0:1] += column_sums(grad_pre)
        part = dot(grad_pre, w_fc1_ref[...], MATMUL_NN)

        @pl.when(block == 0)
        def _():
            total_ref[slot] = part

        @pl.when(block != 0)
        def _():
            total_ref[slot] += part

        return carry

    lax.fori_loop(0, slots, rows, 0)
    step = 2 * LANES
    hidden = hidden_ref[...].reshape(slots * padded, width)
    normed = normed_ref[...].reshape(slots * padded, width)
    for at in range(0, width, step):
        grad_fc2_ref[0, at : at + step, :] = dot(
            branch_ref[:, at : at + step], hidden, MATMUL_TN
        ).astype(jnp.bfloat16)
        grad_fc1_ref[at : at + step, :] = dot(
            pre_ref[:, at : at + step], normed, MATMUL_TN
        ).astype(jnp.bfloat16)

    @pl.when(block == pl.num_programs(0) - 1)
    def _():
        def last(slot, carry):
            grad_normed = total_ref[slot]
            scaled, inv_std = norm_parts(middle_ref[slot])
            sums_ref[0:1] += column_sums(grad_normed * scaled)
            sums_ref[1:2] += column_sums(grad_normed)
            out_ref[slot] = grad_ref[slot] + norm_back(
                grad_normed, scaled, inv_std, gains_ref[1:2]
            )
            return carry

        lax.fori_loop(0, slots, last, 0)


def mlp_backward(grad, middle, normed, hidden, slope, w_fc1, w_fc2, gains):
    slots, padded, width = grad.shape
    blocks = w_fc2.shape[0]
    outs = [
        jax.ShapeDtypeStruct(w_fc1.shape, jnp.bfloat16),
        jax.ShapeDtypeStruct(w_fc2.shape, jnp.bfloat16),
        jax.ShapeDtypeStruct((blocks, 8, width), jnp.float32),
        jax.ShapeDtypeStruct((8, width), jnp.float32),
        jax.ShapeDtypeStruct(grad.shape, jnp.float32),
    ]
    wide_spec = pl.BlockSpec((slots, padded, width), lambda i: (0, 0, i))
    fc1_spec = pl.BlockSpec((width, width), lambda i: (i, 0))
    fc2_spec = pl.BlockSpec((1, width, width), lambda i: (i, 0, 0))
    return pl.pallas_call(
        mlp_backward_kernel,
        grid=(blocks,),
        in_specs=[whole(grad.shape), whole(grad.shape), whole(grad.shape)]
        + [wide_spec, wide_spec, fc1_spec, fc2_spec, whole(gains.shape)],
        out_specs=[
            fc1_spec,
            fc2_spec,
            pl.BlockSpec((1, 8, width), lambda i: (i, 0, 0)),
            whole((8, width)),
            whole(grad.shape),
        ],
        out_shape=outs,
        scratch_shapes=[
            pltpu.VMEM((slots * padded, width), jnp.bfloat16),
            pltpu.VMEM((slots * padded, width), jnp.bfloat16),
            pltpu.VMEM(grad.shape, jnp.float32),
        ],
        compiler_params=params(),
        cost_estimate=worth(34),
        name="mlp_backward",
    )(grad, middle, normed, hidden, slope, w_fc1, w_fc2, gains)


def attn_backward_kernel(grad_ref, x_ref, normed_ref, mixed_ref, probs_ref, attended_ref,
                         w_qkv_ref, w_proj_ref, gains_ref,
                         grad_qkv_ref, grad_proj_ref, sums_ref, out_ref,
                         mixed_all, normed_all, attended_all, branch_all):
    slot = pl.program_id(0)
    _, padded, width = grad_ref.shape
    here = pl.ds(pl.multiple_of(slot * padded, TILE_ROWS), padded)

    @pl.when(slot == 0)
    def _():
        sums_ref[...] = jnp.zeros_like(sums_ref)

    branch = grad_ref[0].astype(jnp.bfloat16)
    branch_all[here, :] = branch
    normed_all[here, :] = normed_ref[0]
    attended_all[here, :] = attended_ref[0]
    grad_attended = dot(branch, w_proj_ref[...], MATMUL_NN).astype(jnp.bfloat16)
    for pair in range(width // LANES):
        at = pair * LANES
        query = mixed_ref[0, :, at : at + LANES]
        key = mixed_ref[0, :, width + at : width + at + LANES]
        value = mixed_ref[0, :, 2 * width + at : 2 * width + at + LANES]
        grad_pair = grad_attended[:, at : at + LANES]
        grad_query = grad_key = grad_value = 0.0
        for side in range(2):
            probs = probs_ref[0, 2 * pair + side]
            wide_probs = probs.astype(jnp.float32)
            grad_side = side_of(grad_pair, side)
            grad_value += dot(probs, grad_side, MATMUL_TN)
            grad_probs = dot(grad_side, value, MATMUL_NT)
            row_inner = jnp.sum(grad_probs * wide_probs, -1, keepdims=True)
            grad_scores = (wide_probs * (grad_probs - row_inner)).astype(jnp.bfloat16)
            grad_query += dot(grad_scores, side_of(key, side), MATMUL_NN)
            grad_key += dot(grad_scores, side_of(query, side), MATMUL_TN)
        grad_query = (grad_query * HEAD_DIM ** (-0.5)).astype(jnp.bfloat16)
        mixed_all[here, at : at + LANES] = grad_query
        mixed_all[here, width + at : width + at + LANES] = grad_key.astype(jnp.bfloat16)
        mixed_all[here, 2 * width + at : 2 * width + at + LANES] = grad_value.astype(jnp.bfloat16)
    grad_mixed = mixed_all[here, :]
    sums_ref[2:3] += column_sums(grad_mixed[:, :width])
    sums_ref[3:4] += column_sums(grad_mixed[:, 2 * width :])
    sums_ref[4:5] += column_sums(branch)
    grad_normed = dot(grad_mixed, w_qkv_ref[...], MATMUL_NN)
    scaled, inv_std = norm_parts(x_ref[0])
    sums_ref[0:1] += column_sums(grad_normed * scaled)
    sums_ref[1:2] += column_sums(grad_normed)
    out_ref[0] = grad_ref[0] + norm_back(grad_normed, scaled, inv_std, gains_ref[0:1])

    @pl.when(slot == pl.num_programs(0) - 1)
    def _():
        step = 2 * LANES
        for at in range(0, 3 * width, step):
            grad_qkv_ref[at : at + step, :] = dot(
                mixed_all[:, at : at + step], normed_all[...], MATMUL_TN
            ).astype(jnp.bfloat16)
        for at in range(0, width, step):
            grad_proj_ref[at : at + step, :] = dot(
                branch_all[:, at : at + step], attended_all[...], MATMUL_TN
            ).astype(jnp.bfloat16)


def attn_backward(grad, state, normed, mixed, probs, attended, w_qkv, w_proj, gains):
    slots, padded, width = grad.shape
    outs = [
        jax.ShapeDtypeStruct(w_qkv.shape, jnp.bfloat16),
        jax.ShapeDtypeStruct(w_proj.shape, jnp.bfloat16),
        jax.ShapeDtypeStruct((8, width), jnp.float32),
        jax.ShapeDtypeStruct(grad.shape, jnp.float32),
    ]
    sliced = (grad, state, normed, mixed, probs, attended)
    return pl.pallas_call(
        attn_backward_kernel,
        grid=(slots,),
        in_specs=[slot_block(v.shape) for v in sliced]
        + [whole(v.shape) for v in (w_qkv, w_proj, gains)],
        out_specs=[whole(o.shape) for o in outs[:3]] + [slot_block(grad.shape)],
        out_shape=outs,
        scratch_shapes=[
            pltpu.VMEM((slots * padded, 3 * width), jnp.bfloat16),
            pltpu.VMEM((slots * padded, width), jnp.bfloat16),
            pltpu.VMEM((slots * padded, width), jnp.bfloat16),
            pltpu.VMEM((slots * padded, width), jnp.bfloat16),
        ],
        compiler_params=params(),
        cost_estimate=worth(29),
        name="attn_backward",
    )(*sliced, w_qkv, w_proj, gains)


AXES = ("dp", "fsdp")


def pack_layer(w_qkv, w_proj, w_fc1, w_fc2, gains, biases, fc1_bias):
    width, tall = w_qkv.shape[0], w_fc2.shape[0]
    cut = w_fc2.T.reshape(w_fc2.shape[1], tall // width, width).transpose(1, 0, 2)
    small = jnp.concatenate([gains.reshape(-1), biases.reshape(-1), fc1_bias.reshape(-1)])
    small = jnp.pad(small, (0, -small.size % width)).reshape(-1, width)
    small = jnp.pad(small, ((0, -small.shape[0] % 16), (0, 0)))
    return jnp.concatenate([w_qkv.T, w_proj.T, w_fc1.T, cut.reshape(-1, width), small], 0)


def unpack_layer(blob, shapes):
    devices, _, width = blob.shape
    qkv, proj, fc1, fc2, gains, biases, fc1_bias = shapes
    at = 0
    parts = []
    for columns in (qkv[1], proj[1], fc1[1]):
        parts.append(blob[:, at : at + columns].reshape(-1, width))
        at += columns
    blocks = fc2[0] // width
    cut = blob[:, at : at + blocks * fc2[1]].reshape(devices, blocks, fc2[1], width)
    parts.append(cut.transpose(1, 0, 2, 3).reshape(blocks, devices * fc2[1], width))
    at += blocks * fc2[1]
    small = blob[:, at:].reshape(devices, -1)
    start = 0
    for rows, columns in (gains, biases, fc1_bias):
        piece = small[:, start : start + rows * columns].reshape(devices, rows, columns)
        piece = piece.transpose(1, 0, 2).astype(jnp.float32)
        parts.append(piece.reshape(rows, devices * columns))
        start += rows * columns
    parts[-1] = parts[-1].reshape(blocks, 1, width)
    return tuple(parts)


def pack_grads(grads, shapes, total_rows, devices):
    grad_qkv, grad_proj, grad_fc1, grad_fc2, gains_grad, biases_grad, fc1_grad = grads
    width = grad_qkv.shape[1]
    qkv, proj, fc1, fc2, gains, biases, fc1_bias = shapes
    blob = jnp.zeros((devices, total_rows, width), jnp.bfloat16)
    at = 0
    for value in (grad_qkv, grad_proj, grad_fc1):
        rows = value.shape[0] // devices
        blob = blob.at[:, at : at + rows].set(
            value.astype(jnp.bfloat16).reshape(devices, rows, width)
        )
        at += rows
    blocks = fc2[0] // width
    cut = grad_fc2.reshape(blocks, devices, fc2[1], width).transpose(1, 0, 2, 3)
    blob = blob.at[:, at : at + blocks * fc2[1]].set(cut.reshape(devices, -1, width))
    at += blocks * fc2[1]
    small = []
    for value, (rows, columns) in ((gains_grad, gains), (biases_grad, biases), (fc1_grad, fc1_bias)):
        small.append(value.reshape(rows, devices, columns).transpose(1, 0, 2).reshape(devices, -1))
    small = jnp.concatenate(small, 1).astype(jnp.bfloat16)
    small = jnp.pad(small, ((0, 0), (0, -small.shape[1] % width))).reshape(devices, -1, width)
    return blob.at[:, at : at + small.shape[1]].set(small)


def unpack_grads(blob, shapes):
    width = blob.shape[1]
    qkv, proj, fc1, fc2, gains, biases, fc1_bias = shapes
    blob = blob.astype(jnp.float32)
    at = 0
    parts = []
    for columns in (qkv[1], proj[1], fc1[1]):
        parts.append(blob[at : at + columns].T)
        at += columns
    blocks = fc2[0] // width
    cut = blob[at : at + blocks * fc2[1]].reshape(blocks, fc2[1], width)
    parts.append(cut.transpose(0, 2, 1).reshape(fc2))
    at += blocks * fc2[1]
    small = blob[at:].reshape(-1)
    start = 0
    for rows, columns in (gains, biases, fc1_bias):
        parts.append(small[start : start + rows * columns].reshape(rows, columns))
        start += rows * columns
    return tuple(parts)


def on_device(images, counts, cotangent, *weights):
    slots, seq_len, width = images.shape
    layer_count = weights[0].shape[0]
    shapes = [w.shape[1:] for w in weights]
    live = (jnp.arange(slots) < counts[0]).astype(jnp.float32)[:, None, None]
    extra = ((0, 0), (0, -seq_len % TILE_ROWS), (0, 0))
    state = jnp.pad(images.astype(jnp.float32), extra)
    gathered = []
    for layer_index in range(layer_count):
        share = pack_layer(*(w[layer_index] for w in weights))
        blob = lax.all_gather(share, AXES, axis=0, tiled=False)
        gathered.append(blob)
    kept = []
    for layer_index in range(layer_count):
        blob, state = lax.optimization_barrier((gathered[layer_index], state))
        gathered[layer_index] = unpack_layer(blob, shapes)
        w_qkv, w_proj, w_fc1, w_fc2, gains, biases, fc1_bias = gathered[layer_index]
        normed_one, mixed, probs, attended, middle = attn_forward(
            state, w_qkv, w_proj, gains, biases, seq_len
        )
        normed_two, hidden, slope, final = mlp_forward(
            middle, w_fc1, w_fc2, gains, biases, fc1_bias
        )
        kept.append((state, normed_one, mixed, probs, attended, middle, normed_two, hidden, slope))
        state = final
    block_output = (state[:, :seq_len] * live).astype(jnp.bfloat16)
    grad_state = jnp.pad(cotangent.astype(jnp.float32) * live, extra)
    layer_grads = [None] * layer_count
    for layer_index in reversed(range(layer_count)):
        w_qkv, w_proj, w_fc1, w_fc2, gains, biases, fc1_bias = gathered[layer_index]
        entry, normed_one, mixed, probs, attended, middle, normed_two, hidden, slope = kept[
            layer_index
        ]
        grad_fc1, grad_fc2, fc1_sums, mlp_sums, grad_middle = mlp_backward(
            grad_state, middle, normed_two, hidden, slope, w_fc1, w_fc2, gains
        )
        grad_qkv, grad_proj, attn_sums, grad_state = attn_backward(
            grad_middle, entry, normed_one, mixed, probs, attended, w_qkv, w_proj, gains
        )
        gains_grad = jnp.stack([attn_sums[0], mlp_sums[0]])
        biases_grad = jnp.stack(
            [attn_sums[1], attn_sums[2], attn_sums[3], attn_sums[4], mlp_sums[1], mlp_sums[2]]
        )
        grads = (
            grad_qkv,
            grad_proj,
            grad_fc1,
            grad_fc2,
            gains_grad,
            biases_grad,
            fc1_sums[:, 0].reshape(1, -1),
        )
        packed = pack_grads(grads, shapes, share.shape[0], blob.shape[0])
        summed = lax.psum_scatter(packed, AXES, scatter_dimension=0, tiled=False)
        layer_grads[layer_index] = unpack_grads(summed, shapes)
    stacked = tuple((jnp.stack([entry[member] for entry in layer_grads]) for member in range(7)))
    return (block_output, grad_state[:, :seq_len], *stacked)


def solution(mesh):
    placed = (
        P(("dp", "fsdp"), None, None),
        P(("dp", "fsdp")),
        P(("dp", "fsdp"), None, None),
        P(None, None, ("dp", "fsdp")),
        P(None, None, ("dp", "fsdp")),
        P(None, None, ("dp", "fsdp")),
        P(None, None, ("dp", "fsdp")),
        P(None, None, ("dp", "fsdp")),
        P(None, None, ("dp", "fsdp")),
        P(None, None, ("dp", "fsdp")),
    )
    return jax.shard_map(
        on_device,
        mesh=mesh,
        in_specs=placed,
        out_specs=(
            P(("dp", "fsdp"), None, None),
            P(("dp", "fsdp"), None, None),
            P(None, None, ("dp", "fsdp")),
            P(None, None, ("dp", "fsdp")),
            P(None, None, ("dp", "fsdp")),
            P(None, None, ("dp", "fsdp")),
            P(None, None, ("dp", "fsdp")),
            P(None, None, ("dp", "fsdp")),
            P(None, None, ("dp", "fsdp")),
        ),
        check_vma=False,
    )
```

```python
import math
from functools import partial

import jax
import jax.numpy as jnp
from jax import lax
from jax.experimental import pallas as pl
from jax.experimental.pallas import tpu as pltpu
from jax.sharding import PartitionSpec as P

HEAD_DIM = 64
MATMUL_NT = (((1,), (1,)), ((), ()))
MATMUL_NN = (((1,), (0,)), ((), ()))
MATMUL_TN = (((0,), (0,)), ((), ()))
VMEM_BYTES = 60 * 1024 * 1024
TILE_ROWS = 16
LANES = 128
SHARE_STEP = 384
BACKWARD_WORTH = 1
MASKED = -1e30


def dot(left, right, dims):
    return lax.dot_general(left, right, dims, preferred_element_type=jnp.float32)


def norm_parts(token_rows):
    row_mean = jnp.mean(token_rows, -1, keepdims=True)
    centered = token_rows - row_mean
    inv_std = lax.rsqrt(jnp.mean(centered * centered, -1, keepdims=True) + 1e-06)
    return (centered * inv_std, inv_std)


def norm_back(grad_normed, scaled, inv_std, gain_row):
    grad_scaled = grad_normed * gain_row
    return inv_std * (
        grad_scaled
        - jnp.mean(grad_scaled, -1, keepdims=True)
        - scaled * jnp.mean(grad_scaled * scaled, -1, keepdims=True)
    )


def column_sums(rows):
    return jnp.sum(rows.astype(jnp.float32), 0, keepdims=True)


def side_of(pair, side):
    lane = lax.broadcasted_iota(jnp.int32, pair.shape, 1)
    mine = (lane >= HEAD_DIM) if side else (lane < HEAD_DIM)
    return jnp.where(mine, pair, jnp.zeros_like(pair))


def put(refs, me_ref, pair, rows, even, odd):
    if len(refs) == 1:
        refs[0][2 * pair, rows, :] = even.astype(jnp.bfloat16)
        refs[0][2 * pair + 1, rows, :] = odd.astype(jnp.bfloat16)
    else:
        place = pair ^ (me_ref[0] >> 1)
        low = (me_ref[0] & 1) == 0
        refs[0][place, rows, :] = jnp.where(low, even, odd).astype(jnp.bfloat16)
        refs[1][place, rows, :] = jnp.where(low, odd, even).astype(jnp.bfloat16)


def share_shapes(mode, devices, rows, width):
    if mode == "joined":
        return [jax.ShapeDtypeStruct((devices, rows, width), jnp.bfloat16)]
    return [jax.ShapeDtypeStruct((devices // 2, rows, width), jnp.bfloat16)] * 2


def attn_forward_kernel(seq_len, x_ref, w_qkv_ref, w_proj_ref, gains_ref, biases_ref,
                        normed_ref, mixed_ref, probs_ref, attended_ref, middle_ref):
    width = x_ref.shape[2]
    token_rows = x_ref[0]
    scaled, _ = norm_parts(token_rows)
    normed = (scaled * gains_ref[0:1] + biases_ref[0:1]).astype(jnp.bfloat16)
    normed_ref[0] = normed
    for part in range(3):
        columns = slice(part * width, (part + 1) * width)
        mixed = dot(normed, w_qkv_ref[columns, :], MATMUL_NT)
        if part == 0:
            mixed = mixed + biases_ref[1:2]
        if part == 2:
            mixed = mixed + biases_ref[2:3]
        mixed = mixed.astype(jnp.bfloat16)
        if part == 0:
            mixed = mixed * jnp.bfloat16(HEAD_DIM ** (-0.5))
        mixed_ref[0, :, columns] = mixed
    padded = x_ref.shape[1]
    real_key = lax.broadcasted_iota(jnp.int32, (padded, padded), 1) < seq_len
    for pair in range(width // LANES):
        at = pair * LANES
        query = mixed_ref[0, :, at : at + LANES]
        key = mixed_ref[0, :, width + at : width + at + LANES]
        value = mixed_ref[0, :, 2 * width + at : 2 * width + at + LANES]
        total = None
        for side in range(2):
            scores = dot(side_of(query, side), key, MATMUL_NT)
            scores = jnp.where(real_key, scores, MASKED)
            top = jnp.max(scores, -1, keepdims=True)
            expo = jnp.exp(scores - top)
            probs = (expo / jnp.sum(expo, -1, keepdims=True)).astype(jnp.bfloat16)
            probs_ref[0, 2 * pair + side] = probs
            part = dot(probs, side_of(value, side), MATMUL_NN)
            total = part if total is None else total + part
        attended_ref[0, :, at : at + LANES] = total.astype(jnp.bfloat16)
    middle_ref[0] = (
        token_rows + dot(attended_ref[0], w_proj_ref[...], MATMUL_NT) + biases_ref[3:4]
    )


def whole(shape):
    return pl.BlockSpec(shape, lambda i: (0,) * len(shape), pipeline_mode=pl.Buffered(1))


def slot_block(shape):
    return pl.BlockSpec((1, *shape[1:]), lambda i: (i,) + (0,) * (len(shape) - 1))


def worth(microseconds):
    return pl.CostEstimate(
        flops=int(microseconds * 1e9), bytes_accessed=1 << 20, transcendentals=0
    )


def params():
    return pltpu.CompilerParams(
        dimension_semantics=("arbitrary",), vmem_limit_bytes=VMEM_BYTES
    )


def attn_forward(state, w_qkv, w_proj, gains, biases, seq_len):
    slots, padded, width = state.shape
    heads = width // HEAD_DIM
    outs = [
        jax.ShapeDtypeStruct((slots, padded, width), jnp.bfloat16),
        jax.ShapeDtypeStruct((slots, padded, 3 * width), jnp.bfloat16),
        jax.ShapeDtypeStruct((slots, heads, padded, padded), jnp.bfloat16),
        jax.ShapeDtypeStruct((slots, padded, width), jnp.bfloat16),
        jax.ShapeDtypeStruct((slots, padded, width), jnp.float32),
    ]
    return pl.pallas_call(
        partial(attn_forward_kernel, seq_len),
        grid=(slots,),
        in_specs=[slot_block(state.shape)]
        + [whole(v.shape) for v in (w_qkv, w_proj, gains, biases)],
        out_specs=[slot_block(o.shape) for o in outs],
        out_shape=outs,
        compiler_params=params(),
        cost_estimate=worth(18),
        name="attn_forward",
    )(state, w_qkv, w_proj, gains, biases)


def mlp_forward_kernel(middle_ref, w_fc1_ref, w_fc2_ref, gains_ref, biases_ref, fc1_bias_ref,
                       normed_ref, hidden_ref, slope_ref, final_ref):
    block = pl.program_id(0)
    slots = middle_ref.shape[0]

    @pl.when(block == 0)
    def _():
        def first(slot, carry):
            middle = middle_ref[slot]
            scaled, _ = norm_parts(middle)
            normed_ref[slot] = (scaled * gains_ref[1:2] + biases_ref[4:5]).astype(jnp.bfloat16)
            final_ref[slot] = middle + biases_ref[5:6]
            return carry

        lax.fori_loop(0, slots, first, 0)

    def rows(slot, carry):
        pre = dot(normed_ref[slot], w_fc1_ref[...], MATMUL_NT) + fc1_bias_ref[0]
        below = 0.5 * (1.0 + lax.erf(pre * 0.5**0.5))
        hidden = (pre * below).astype(jnp.bfloat16)
        bell = jnp.exp(-0.5 * (pre * pre)) * (2.0 * math.pi) ** -0.5
        slope_ref[slot] = (below + pre * bell).astype(jnp.bfloat16)
        hidden_ref[slot] = hidden
        final_ref[slot] += dot(hidden, w_fc2_ref[0], MATMUL_NT)
        return carry

    lax.fori_loop(0, slots, rows, 0)


def mlp_forward(middle, w_fc1, w_fc2, gains, biases, fc1_bias):
    slots, padded, width = middle.shape
    blocks = w_fc2.shape[0]
    wide = (slots, padded, blocks * width)
    outs = [
        jax.ShapeDtypeStruct(middle.shape, jnp.bfloat16),
        jax.ShapeDtypeStruct(wide, jnp.bfloat16),
        jax.ShapeDtypeStruct(wide, jnp.bfloat16),
        jax.ShapeDtypeStruct(middle.shape, jnp.float32),
    ]
    wide_spec = pl.BlockSpec((slots, padded, width), lambda i: (0, 0, i))
    return pl.pallas_call(
        mlp_forward_kernel,
        grid=(blocks,),
        in_specs=[
            whole(middle.shape),
            pl.BlockSpec((width, width), lambda i: (i, 0)),
            pl.BlockSpec((1, width, width), lambda i: (i, 0, 0)),
            whole(gains.shape),
            whole(biases.shape),
            pl.BlockSpec((1, 1, width), lambda i: (i, 0, 0)),
        ],
        out_specs=[whole(middle.shape), wide_spec, wide_spec, whole(middle.shape)],
        out_shape=outs,
        compiler_params=params(),
        cost_estimate=worth(24),
        name="mlp_forward",
    )(middle, w_fc1, w_fc2, gains, biases, fc1_bias)


def mlp_backward_kernel(mode, cut, me_ref, grad_ref, middle_ref, normed_ref, hidden_ref, slope_ref, w_fc1_ref,
                        w_fc2_ref, gains_ref, *refs):
    share_count = 1 if mode == "joined" else 2
    share_refs = refs[:share_count]
    fc1_sums_ref, sums_ref, out_ref, branch_ref, pre_ref, total_ref, before_ref = refs[share_count:]
    block = pl.program_id(0)
    slots, padded, width = grad_ref.shape

    @pl.when(block == 0)
    def _():
        sums_ref[...] = jnp.zeros_like(sums_ref)

        def first(slot, carry):
            branch = grad_ref[slot].astype(jnp.bfloat16)
            branch_ref[pl.ds(pl.multiple_of(slot * padded, TILE_ROWS), padded), :] = branch
            sums_ref[2:3] += column_sums(branch)
            return carry

        lax.fori_loop(0, slots, first, 0)

    fc1_sums_ref[...] = jnp.zeros_like(fc1_sums_ref)

    def rows(slot, carry):
        here = pl.ds(pl.multiple_of(slot * padded, TILE_ROWS), padded)
        grad_hidden = dot(branch_ref[here, :], w_fc2_ref[0], MATMUL_NN)
        grad_pre = (grad_hidden * slope_ref[slot].astype(jnp.float32)).astype(jnp.bfloat16)
        pre_ref[here, :] = grad_pre
        fc1_sums_ref[0, 0:1] += column_sums(grad_pre)
        part = dot(grad_pre, w_fc1_ref[...], MATMUL_NN)

        @pl.when(block == 0)
        def _():
            total_ref[slot] = part

        @pl.when(block != 0)
        def _():
            total_ref[slot] += part

        return carry

    lax.fori_loop(0, slots, rows, 0)
    hidden = hidden_ref[...].reshape(slots * padded, width)
    normed = normed_ref[...].reshape(slots * padded, width)
    if mode == "plain":
        grad_fc1_ref, grad_fc2_ref = share_refs
        step = 2 * LANES
        for at in range(0, width, step):
            grad_fc2_ref[0, at : at + step, :] = dot(
                branch_ref[:, at : at + step], hidden, MATMUL_TN
            ).astype(jnp.bfloat16)
            grad_fc1_ref[at : at + step, :] = dot(
                pre_ref[:, at : at + step], normed, MATMUL_TN
            ).astype(jnp.bfloat16)
    else:
        tall = 4 * cut
        for at in range(0, width, SHARE_STEP):
            value = dot(pre_ref[:, at : at + SHARE_STEP], normed, MATMUL_TN)
            value = value.reshape(SHARE_STEP // tall, tall, width)
            for s in range(0, SHARE_STEP // tall, 2):
                pair = block * (width // tall // 2) + at // tall // 2 + s // 2
                put(share_refs, me_ref, pair, slice(0, tall), value[s], value[s + 1])
            value = dot(branch_ref[:, at : at + SHARE_STEP], hidden, MATMUL_TN)

            @pl.when(block % 2 == 0)
            def _():
                before_ref[at : at + SHARE_STEP, :] = value

            for odd in range(1, 4, 2):

                @pl.when(block == odd)
                def _():
                    before = before_ref[at : at + SHARE_STEP, :].reshape(-1, cut, width)
                    both = jnp.concatenate([before, value.reshape(-1, cut, width)], 1)
                    rows = slice(tall + (odd - 1) * cut, tall + (odd + 1) * cut)
                    for s in range(0, SHARE_STEP // cut, 2):
                        pair = at // cut // 2 + s // 2
                        put(share_refs, me_ref, pair, rows, both[s], both[s + 1])

    @pl.when(block == pl.num_programs(0) - 1)
    def _():
        def last(slot, carry):
            grad_normed = total_ref[slot]
            scaled, inv_std = norm_parts(middle_ref[slot])
            sums_ref[0:1] += column_sums(grad_normed * scaled)
            sums_ref[1:2] += column_sums(grad_normed)
            out_ref[slot] = grad_ref[slot] + norm_back(
                grad_normed, scaled, inv_std, gains_ref[1:2]
            )
            return carry

        lax.fori_loop(0, slots, last, 0)


def mlp_backward(mode, devices, me, grad, middle, normed, hidden, slope, w_fc1, w_fc2, gains):
    slots, padded, width = grad.shape
    blocks = w_fc2.shape[0]
    cut = width // devices
    fc1_spec = pl.BlockSpec((width, width), lambda i: (i, 0))
    fc2_spec = pl.BlockSpec((1, width, width), lambda i: (i, 0, 0))
    if mode == "plain":
        shares = [jax.ShapeDtypeStruct(v.shape, jnp.bfloat16) for v in (w_fc1, w_fc2)]
        share_specs = [fc1_spec, fc2_spec]
    else:
        shares = share_shapes(mode, devices, 8 * cut, width)
        share_specs = [whole(v.shape) for v in shares]
    outs = shares + [
        jax.ShapeDtypeStruct((blocks, 8, width), jnp.float32),
        jax.ShapeDtypeStruct((8, width), jnp.float32),
        jax.ShapeDtypeStruct(grad.shape, jnp.float32),
    ]
    wide_spec = pl.BlockSpec((slots, padded, width), lambda i: (0, 0, i))
    return pl.pallas_call(
        partial(mlp_backward_kernel, mode, cut),
        grid=(blocks,),
        in_specs=[pl.BlockSpec(memory_space=pltpu.SMEM)]
        + [whole(grad.shape), whole(grad.shape), whole(grad.shape)]
        + [wide_spec, wide_spec, fc1_spec, fc2_spec, whole(gains.shape)],
        out_specs=share_specs
        + [
            pl.BlockSpec((1, 8, width), lambda i: (i, 0, 0)),
            whole((8, width)),
            whole(grad.shape),
        ],
        out_shape=outs,
        scratch_shapes=[
            pltpu.VMEM((slots * padded, width), jnp.bfloat16),
            pltpu.VMEM((slots * padded, width), jnp.bfloat16),
            pltpu.VMEM(grad.shape, jnp.float32),
            pltpu.VMEM((width, width), jnp.float32),
        ],
        compiler_params=params(),
        cost_estimate=worth(BACKWARD_WORTH),
        name="mlp_backward",
    )(me, grad, middle, normed, hidden, slope, w_fc1, w_fc2, gains)


def attn_backward_kernel(mode, cut, me_ref, grad_ref, x_ref, normed_ref, mixed_ref, probs_ref, attended_ref,
                         w_qkv_ref, w_proj_ref, gains_ref, *refs):
    share_count = 1 if mode == "joined" else 2
    share_refs = refs[:share_count]
    sums_ref, out_ref, mixed_all, normed_all, attended_all, branch_all = refs[share_count:]
    slot = pl.program_id(0)
    _, padded, width = grad_ref.shape
    here = pl.ds(pl.multiple_of(slot * padded, TILE_ROWS), padded)

    @pl.when(slot == 0)
    def _():
        sums_ref[...] = jnp.zeros_like(sums_ref)

    branch = grad_ref[0].astype(jnp.bfloat16)
    branch_all[here, :] = branch
    normed_all[here, :] = normed_ref[0]
    attended_all[here, :] = attended_ref[0]
    grad_attended = dot(branch, w_proj_ref[...], MATMUL_NN).astype(jnp.bfloat16)
    for pair in range(width // LANES):
        at = pair * LANES
        query = mixed_ref[0, :, at : at + LANES]
        key = mixed_ref[0, :, width + at : width + at + LANES]
        value = mixed_ref[0, :, 2 * width + at : 2 * width + at + LANES]
        grad_pair = grad_attended[:, at : at + LANES]
        grad_query = grad_key = grad_value = 0.0
        for side in range(2):
            probs = probs_ref[0, 2 * pair + side]
            wide_probs = probs.astype(jnp.float32)
            grad_side = side_of(grad_pair, side)
            grad_value += dot(probs, grad_side, MATMUL_TN)
            grad_probs = dot(grad_side, value, MATMUL_NT)
            row_inner = jnp.sum(grad_probs * wide_probs, -1, keepdims=True)
            grad_scores = (wide_probs * (grad_probs - row_inner)).astype(jnp.bfloat16)
            grad_query += dot(grad_scores, side_of(key, side), MATMUL_NN)
            grad_key += dot(grad_scores, side_of(query, side), MATMUL_TN)
        grad_query = (grad_query * HEAD_DIM ** (-0.5)).astype(jnp.bfloat16)
        mixed_all[here, at : at + LANES] = grad_query
        mixed_all[here, width + at : width + at + LANES] = grad_key.astype(jnp.bfloat16)
        mixed_all[here, 2 * width + at : 2 * width + at + LANES] = grad_value.astype(jnp.bfloat16)
    grad_mixed = mixed_all[here, :]
    sums_ref[2:3] += column_sums(grad_mixed[:, :width])
    sums_ref[3:4] += column_sums(grad_mixed[:, 2 * width :])
    sums_ref[4:5] += column_sums(branch)
    grad_normed = dot(grad_mixed, w_qkv_ref[...], MATMUL_NN)
    scaled, inv_std = norm_parts(x_ref[0])
    sums_ref[0:1] += column_sums(grad_normed * scaled)
    sums_ref[1:2] += column_sums(grad_normed)
    out_ref[0] = grad_ref[0] + norm_back(grad_normed, scaled, inv_std, gains_ref[0:1])

    @pl.when(slot == pl.num_programs(0) - 1)
    def _():
        if mode == "plain":
            grad_qkv_ref, grad_proj_ref = share_refs
            step = 2 * LANES
            for at in range(0, 3 * width, step):
                grad_qkv_ref[at : at + step, :] = dot(
                    mixed_all[:, at : at + step], normed_all[...], MATMUL_TN
                ).astype(jnp.bfloat16)
            for at in range(0, width, step):
                grad_proj_ref[at : at + step, :] = dot(
                    branch_all[:, at : at + step], attended_all[...], MATMUL_TN
                ).astype(jnp.bfloat16)
        else:
            for at in range(0, width, SHARE_STEP):
                three = slice(3 * at, 3 * (at + SHARE_STEP))
                value = dot(mixed_all[:, three], normed_all[...], MATMUL_TN)
                more = dot(
                    branch_all[:, at : at + SHARE_STEP], attended_all[...], MATMUL_TN
                )
                both = jnp.concatenate(
                    [value.reshape(-1, 3 * cut, width), more.reshape(-1, cut, width)], 1
                )
                for s in range(0, SHARE_STEP // cut, 2):
                    pair = at // cut // 2 + s // 2
                    put(share_refs, me_ref, pair, slice(0, 4 * cut), both[s], both[s + 1])


def attn_backward(mode, devices, me, grad, state, normed, mixed, probs, attended, w_qkv, w_proj, gains, length):
    slots, padded, width = grad.shape
    cut = width // devices
    if mode == "plain":
        shares = [jax.ShapeDtypeStruct(v.shape, jnp.bfloat16) for v in (w_qkv, w_proj)]
    else:
        shares = share_shapes(mode, devices, 4 * cut + TILE_ROWS, width)
    outs = shares + [
        jax.ShapeDtypeStruct((8, width), jnp.float32),
        jax.ShapeDtypeStruct(grad.shape, jnp.float32),
    ]
    sliced = (grad, state, normed, mixed, probs, attended)
    return pl.pallas_call(
        partial(attn_backward_kernel, mode, cut),
        grid=(slots,),
        in_specs=[pl.BlockSpec(memory_space=pltpu.SMEM)]
        + [slot_block(v.shape) for v in sliced]
        + [whole(v.shape) for v in (w_qkv, w_proj, gains)],
        out_specs=[whole(o.shape) for o in outs[:-1]] + [slot_block(grad.shape)],
        out_shape=outs,
        scratch_shapes=[
            pltpu.VMEM((slots * padded, 3 * width), jnp.bfloat16),
            pltpu.VMEM((slots * padded, width), jnp.bfloat16),
            pltpu.VMEM((slots * padded, width), jnp.bfloat16),
            pltpu.VMEM((slots * padded, width), jnp.bfloat16),
        ],
        compiler_params=params(),
        cost_estimate=worth(length),
        name="attn_backward",
    )(me, *sliced, w_qkv, w_proj, gains)


AXES = ("dp", "fsdp")


def pack_layer(w_qkv, w_proj, w_fc1, w_fc2, gains, biases, fc1_bias):
    width, tall = w_qkv.shape[0], w_fc2.shape[0]
    cut = w_fc2.T.reshape(w_fc2.shape[1], tall // width, width).transpose(1, 0, 2)
    small = jnp.concatenate([gains.reshape(-1), biases.reshape(-1), fc1_bias.reshape(-1)])
    small = jnp.pad(small, (0, -small.size % width)).reshape(-1, width)
    small = jnp.pad(small, ((0, -small.shape[0] % 16), (0, 0)))
    return jnp.concatenate([w_qkv.T, w_proj.T, w_fc1.T, cut.reshape(-1, width), small], 0)


def unpack_layer(blob, shapes):
    devices, _, width = blob.shape
    qkv, proj, fc1, fc2, gains, biases, fc1_bias = shapes
    at = 0
    parts = []
    for columns in (qkv[1], proj[1], fc1[1]):
        parts.append(blob[:, at : at + columns].reshape(-1, width))
        at += columns
    blocks = fc2[0] // width
    cut = blob[:, at : at + blocks * fc2[1]].reshape(devices, blocks, fc2[1], width)
    parts.append(cut.transpose(1, 0, 2, 3).reshape(blocks, devices * fc2[1], width))
    at += blocks * fc2[1]
    small = blob[:, at:].reshape(devices, -1)
    start = 0
    for rows, columns in (gains, biases, fc1_bias):
        piece = small[:, start : start + rows * columns].reshape(devices, rows, columns)
        piece = piece.transpose(1, 0, 2).astype(jnp.float32)
        parts.append(piece.reshape(rows, devices * columns))
        start += rows * columns
    parts[-1] = parts[-1].reshape(blocks, 1, width)
    return tuple(parts)


def pack_grads(grads, shapes, total_rows, devices):
    grad_qkv, grad_proj, grad_fc1, grad_fc2, gains_grad, biases_grad, fc1_grad = grads
    width = grad_qkv.shape[1]
    qkv, proj, fc1, fc2, gains, biases, fc1_bias = shapes
    blob = jnp.zeros((devices, total_rows, width), jnp.bfloat16)
    at = 0
    for value in (grad_qkv, grad_proj, grad_fc1):
        rows = value.shape[0] // devices
        blob = blob.at[:, at : at + rows].set(
            value.astype(jnp.bfloat16).reshape(devices, rows, width)
        )
        at += rows
    blocks = fc2[0] // width
    cut = grad_fc2.reshape(blocks, devices, fc2[1], width).transpose(1, 0, 2, 3)
    blob = blob.at[:, at : at + blocks * fc2[1]].set(cut.reshape(devices, -1, width))
    at += blocks * fc2[1]
    small = []
    for value, (rows, columns) in ((gains_grad, gains), (biases_grad, biases), (fc1_grad, fc1_bias)):
        small.append(value.reshape(rows, devices, columns).transpose(1, 0, 2).reshape(devices, -1))
    small = jnp.concatenate(small, 1).astype(jnp.bfloat16)
    small = jnp.pad(small, ((0, 0), (0, -small.shape[1] % width))).reshape(devices, -1, width)
    return blob.at[:, at : at + small.shape[1]].set(small)


def unpack_grads(blob, shapes):
    width = blob.shape[1]
    qkv, proj, fc1, fc2, gains, biases, fc1_bias = shapes
    blob = blob.astype(jnp.float32)
    at = 0
    parts = []
    for columns in (qkv[1], proj[1], fc1[1]):
        parts.append(blob[at : at + columns].T)
        at += columns
    blocks = fc2[0] // width
    cut = blob[at : at + blocks * fc2[1]].reshape(blocks, fc2[1], width)
    parts.append(cut.transpose(0, 2, 1).reshape(fc2))
    at += blocks * fc2[1]
    small = blob[at:].reshape(-1)
    start = 0
    for rows, columns in (gains, biases, fc1_bias):
        parts.append(small[start : start + rows * columns].reshape(rows, columns))
        start += rows * columns
    return tuple(parts)


def small_shares(values, devices):
    cut = [v.reshape(v.shape[0], devices, -1).transpose(1, 0, 2) for v in values]
    return jnp.concatenate([v.reshape(devices, -1) for v in cut], 1).astype(jnp.bfloat16)


def small_rows(row, width):
    row = jnp.pad(row, ((0, 0), (0, -row.shape[1] % (TILE_ROWS * width))))
    return row.reshape(row.shape[0], -1, width)


def swap(value, axis, mask, size):
    return lax.ppermute(value, axis, [(i, i ^ mask) for i in range(size)])


def total_of(values):
    return sum(v.astype(jnp.float32) for v in values).astype(jnp.bfloat16)


class Exchange:
    def __init__(self, mine, other, fsdp_size, orders):
        rows, width = mine.shape[-2:]
        self.fsdp_size = fsdp_size
        self.orders = [list(order) for order in orders]
        self.kept = mine
        self.shape = (2, 2, fsdp_size // 2, rows // len(orders), width)
        self.pending = None if other is None else [[swap(other, "fsdp", 1, fsdp_size)]]

    def sums(self):
        if self.pending is None:
            return [self.kept]
        if isinstance(self.kept, list):
            return [total_of([k, *got]) for k, got in zip(self.kept, self.pending)]
        got = self.pending[0][0]
        rows = self.shape[3]
        cuts = [slice(i * rows, (i + 1) * rows) for i in range(len(self.orders))]
        return [total_of([self.kept[:, c], got[:, c]]).reshape(self.shape) for c in cuts]

    def step(self):
        kept, pending = [], []
        for value, order in zip(self.sums(), self.orders):
            stage = order.pop(0)
            if stage == "z":
                kept.append(value[:, :, :1])
                pending.append(
                    [
                        swap(value[:, :, i : i + 1], "fsdp", 2 * i, self.fsdp_size)
                        for i in range(1, self.fsdp_size // 2)
                    ]
                )
            elif stage == "x":
                kept.append(value[:, :1])
                pending.append([swap(value[:, 1:], "dp", 1, 4)])
            elif stage == "y":
                kept.append(value[:1])
                pending.append([swap(value[1:], "dp", 2, 4)])
            else:
                kept.append(value[:1, :1])
                pending.append(
                    [
                        swap(value[i // 2 : i // 2 + 1, i % 2 : i % 2 + 1], "dp", i, 4)
                        for i in range(1, 4)
                    ]
                )
        self.kept, self.pending = kept, pending

    def result(self):
        return jnp.concatenate([v.reshape(self.shape[3:]) for v in self.sums()], 0)


def gate(values, *exchanges):
    values, arrived = lax.optimization_barrier((values, [e.pending for e in exchanges]))
    for exchange, pending in zip(exchanges, arrived):
        exchange.pending = pending
    return values


HALVES = (("x", "y"), ("y", "x"))
WHOLE = (("xy", "z"),)


def on_device(dp_size, fsdp_size, images, counts, cotangent, *weights):
    slots, seq_len, width = images.shape
    layer_count = weights[0].shape[0]
    shapes = [w.shape[1:] for w in weights]
    devices = dp_size * fsdp_size
    cut = width // devices
    direct = dp_size == 4 and layer_count == 2 and cut % 8 == 0 and SHARE_STEP % (8 * cut) == 0 and devices * cut == width
    live = (jnp.arange(slots) < counts[0]).astype(jnp.float32)[:, None, None]
    me = lax.axis_index("dp") * fsdp_size + lax.axis_index("fsdp")
    place = jnp.arange(devices)
    place = (jnp.bitwise_xor(2 * (place % (devices // 2)) + place // (devices // 2), me))[:, None]
    relative = (place == jnp.arange(devices)[None]).astype(jnp.bfloat16)
    me = me.astype(jnp.int32).reshape(1)
    extra = ((0, 0), (0, -seq_len % TILE_ROWS), (0, 0))
    state = jnp.pad(images.astype(jnp.float32), extra)
    gathered = []
    for layer_index in range(layer_count):
        share = pack_layer(*(w[layer_index] for w in weights))
        blob = lax.all_gather(share, AXES, axis=0, tiled=False)
        gathered.append(blob)
    kept = []
    for layer_index in range(layer_count):
        blob, state = lax.optimization_barrier((gathered[layer_index], state))
        gathered[layer_index] = unpack_layer(blob, shapes)
        w_qkv, w_proj, w_fc1, w_fc2, gains, biases, fc1_bias = gathered[layer_index]
        normed_one, mixed, probs, attended, middle = attn_forward(
            state, w_qkv, w_proj, gains, biases, seq_len
        )
        normed_two, hidden, slope, final = mlp_forward(
            middle, w_fc1, w_fc2, gains, biases, fc1_bias
        )
        kept.append((state, normed_one, mixed, probs, attended, middle, normed_two, hidden, slope))
        state = final
    block_output = (state[:, :seq_len] * live).astype(jnp.bfloat16)
    grad_state = jnp.pad(cotangent.astype(jnp.float32) * live, extra)
    layer_grads = [None] * layer_count

    def small_of(mlp, attn):
        fc1_sums, mlp_sums = mlp
        gains_grad = jnp.stack([attn[0], mlp_sums[0]])
        biases_grad = jnp.stack([attn[1], attn[2], attn[3], attn[4], mlp_sums[1], mlp_sums[2]])
        return (gains_grad, biases_grad, fc1_sums[:, 0].reshape(1, -1))

    def mlp_part(layer_index, mode, grad_state):
        w_fc1, w_fc2, gains = gathered[layer_index][2:5]
        middle, normed, hidden, slope = kept[layer_index][5:]
        *shares, fc1_sums, sums, grad_middle = mlp_backward(
            mode, devices, me, grad_state, middle, normed, hidden, slope, w_fc1, w_fc2, gains
        )
        return shares, (fc1_sums, sums), grad_middle

    def attn_part(layer_index, mode, grad_middle):
        w_qkv, w_proj, gains = (gathered[layer_index][i] for i in (0, 1, 4))
        *shares, sums, grad_state = attn_backward(
            mode, devices, me, grad_middle, *kept[layer_index][:5], w_qkv, w_proj, gains,
            1 if layer_index else 200
        )
        return shares, sums, grad_state

    def with_small(shares, mlp, attn):
        row = small_shares(small_of(mlp, attn), devices)
        row = jnp.dot(relative, row, preferred_element_type=jnp.float32).astype(jnp.bfloat16)
        row = small_rows(row, width)
        count = shares[0].shape[0]
        return [v.at[:, 4 * cut :].set(row[i * count : (i + 1) * count]) for i, v in enumerate(shares)]

    def owned(attn_sum, mlp_sum):
        summed = jnp.concatenate([attn_sum[: 4 * cut], mlp_sum, attn_sum[4 * cut :]], 0)
        return unpack_grads(summed, shapes)

    if direct:
        shares, mlp, grad_middle = mlp_part(1, "split", grad_state)
        mlp_one = Exchange(*shares, fsdp_size, HALVES)
        shares, attn, grad_state = attn_part(1, "split", grad_middle)
        shares, attn, grad_state = gate((shares, attn, grad_state), mlp_one)
        mlp_one.step()
        attn_one = Exchange(*with_small(shares, mlp, attn), fsdp_size, WHOLE)
        shares, mlp, grad_middle = mlp_part(0, "joined", grad_state)
        mlp_zero = lax.psum_scatter(shares[0], AXES, scatter_dimension=0, tiled=False)
        grad_middle, mlp = gate((grad_middle, mlp), mlp_one, attn_one)
        mlp_one.step()
        attn_one.step()
        shares, attn, grad_state = attn_part(0, "split", grad_middle)
        shares, attn, grad_state = gate((shares, attn, grad_state), mlp_one, attn_one)
        late = mlp_one.sums() + attn_one.sums()
        late = Exchange(jnp.concatenate(late, 3), None, fsdp_size, (("z",),))
        late.step()
        attn_zero = Exchange(*with_small(shares, mlp, attn), fsdp_size, WHOLE)
        attn_zero.step()
        arrived = attn_zero.pending
        late.pending, arrived = lax.optimization_barrier((late.pending, arrived))
        attn_zero.step()
        late = late.result()
        layer_grads[1] = owned(late[8 * cut :], late[: 8 * cut])
        layer_grads[0] = owned(attn_zero.result(), mlp_zero)
    else:
        for layer_index in reversed(range(layer_count)):
            mlp_shares, mlp, grad_middle = mlp_part(layer_index, "plain", grad_state)
            attn_shares, attn, grad_state = attn_part(layer_index, "plain", grad_middle)
            grads = (*attn_shares, *mlp_shares, *small_of(mlp, attn))
            packed = pack_grads(grads, shapes, share.shape[0], devices)
            summed = lax.psum_scatter(packed, AXES, scatter_dimension=0, tiled=False)
            layer_grads[layer_index] = unpack_grads(summed, shapes)
    stacked = tuple((jnp.stack([entry[member] for entry in layer_grads]) for member in range(7)))
    return (block_output, grad_state[:, :seq_len], *stacked)


def solution(mesh):
    placed = (
        P(("dp", "fsdp"), None, None),
        P(("dp", "fsdp")),
        P(("dp", "fsdp"), None, None),
        P(None, None, ("dp", "fsdp")),
        P(None, None, ("dp", "fsdp")),
        P(None, None, ("dp", "fsdp")),
        P(None, None, ("dp", "fsdp")),
        P(None, None, ("dp", "fsdp")),
        P(None, None, ("dp", "fsdp")),
        P(None, None, ("dp", "fsdp")),
    )
    return jax.shard_map(
        partial(on_device, mesh.shape["dp"], mesh.shape["fsdp"]),
        mesh=mesh,
        in_specs=placed,
        out_specs=(
            P(("dp", "fsdp"), None, None),
            P(("dp", "fsdp"), None, None),
            P(None, None, ("dp", "fsdp")),
            P(None, None, ("dp", "fsdp")),
            P(None, None, ("dp", "fsdp")),
            P(None, None, ("dp", "fsdp")),
            P(None, None, ("dp", "fsdp")),
            P(None, None, ("dp", "fsdp")),
            P(None, None, ("dp", "fsdp")),
        ),
        check_vma=False,
    )
```

```python
import math
from functools import partial

import jax
import jax.numpy as jnp
from jax import lax
from jax.experimental import pallas as pl
from jax.experimental.pallas import tpu as pltpu
from jax.sharding import PartitionSpec as P

HEAD_DIM = 64
MATMUL_NT = (((1,), (1,)), ((), ()))
MATMUL_NN = (((1,), (0,)), ((), ()))
MATMUL_TN = (((0,), (0,)), ((), ()))
VMEM_BYTES = 60 * 1024 * 1024
TILE_ROWS = 16
LANES = 128
SHARE_STEP = 384
BACKWARD_WORTH = 1
MASKED = -1e30


def dot(left, right, dims):
    return lax.dot_general(left, right, dims, preferred_element_type=jnp.float32)


def norm_parts(token_rows):
    row_mean = jnp.mean(token_rows, -1, keepdims=True)
    centered = token_rows - row_mean
    inv_std = lax.rsqrt(jnp.mean(centered * centered, -1, keepdims=True) + 1e-06)
    return (centered * inv_std, inv_std)


def norm_back(grad_normed, scaled, inv_std, gain_row):
    grad_scaled = grad_normed * gain_row
    return inv_std * (
        grad_scaled
        - jnp.mean(grad_scaled, -1, keepdims=True)
        - scaled * jnp.mean(grad_scaled * scaled, -1, keepdims=True)
    )


def column_sums(rows):
    return jnp.sum(rows.astype(jnp.float32), 0, keepdims=True)


def side_of(pair, side):
    lane = lax.broadcasted_iota(jnp.int32, pair.shape, 1)
    mine = (lane >= HEAD_DIM) if side else (lane < HEAD_DIM)
    return jnp.where(mine, pair, jnp.zeros_like(pair))


def put(refs, me_ref, pair, rows, even, odd):
    if len(refs) == 1:
        refs[0][2 * pair, rows, :] = even.astype(jnp.bfloat16)
        refs[0][2 * pair + 1, rows, :] = odd.astype(jnp.bfloat16)
    else:
        place = pair ^ (me_ref[0] >> 1)
        low = (me_ref[0] & 1) == 0
        refs[0][place, rows, :] = jnp.where(low, even, odd).astype(jnp.bfloat16)
        refs[1][place, rows, :] = jnp.where(low, odd, even).astype(jnp.bfloat16)


def share_shapes(mode, devices, rows, width):
    if mode == "joined":
        return [jax.ShapeDtypeStruct((devices, rows, width), jnp.bfloat16)]
    return [jax.ShapeDtypeStruct((devices // 2, rows, width), jnp.bfloat16)] * 2


def attn_forward_kernel(seq_len, x_ref, w_qkv_ref, w_proj_ref, gains_ref, biases_ref,
                        normed_ref, mixed_ref, probs_ref, attended_ref, middle_ref):
    width = x_ref.shape[2]
    token_rows = x_ref[0]
    scaled, _ = norm_parts(token_rows)
    normed = (scaled * gains_ref[0:1] + biases_ref[0:1]).astype(jnp.bfloat16)
    normed_ref[0] = normed
    for part in range(3):
        columns = slice(part * width, (part + 1) * width)
        mixed = dot(normed, w_qkv_ref[columns, :], MATMUL_NT)
        if part == 0:
            mixed = mixed + biases_ref[1:2]
        if part == 2:
            mixed = mixed + biases_ref[2:3]
        mixed = mixed.astype(jnp.bfloat16)
        if part == 0:
            mixed = mixed * jnp.bfloat16(HEAD_DIM ** (-0.5))
        mixed_ref[0, :, columns] = mixed
    padded = x_ref.shape[1]
    real_key = lax.broadcasted_iota(jnp.int32, (padded, padded), 1) < seq_len
    for pair in range(width // LANES):
        at = pair * LANES
        query = mixed_ref[0, :, at : at + LANES]
        key = mixed_ref[0, :, width + at : width + at + LANES]
        value = mixed_ref[0, :, 2 * width + at : 2 * width + at + LANES]
        total = None
        for side in range(2):
            scores = dot(side_of(query, side), key, MATMUL_NT)
            scores = jnp.where(real_key, scores, MASKED)
            top = jnp.max(scores, -1, keepdims=True)
            expo = jnp.exp(scores - top)
            probs = (expo / jnp.sum(expo, -1, keepdims=True)).astype(jnp.bfloat16)
            probs_ref[0, 2 * pair + side] = probs
            part = dot(probs, side_of(value, side), MATMUL_NN)
            total = part if total is None else total + part
        attended_ref[0, :, at : at + LANES] = total.astype(jnp.bfloat16)
    middle_ref[0] = (
        token_rows + dot(attended_ref[0], w_proj_ref[...], MATMUL_NT) + biases_ref[3:4]
    )


def whole(shape):
    return pl.BlockSpec(shape, lambda i: (0,) * len(shape), pipeline_mode=pl.Buffered(1))


def slot_block(shape):
    return pl.BlockSpec((1, *shape[1:]), lambda i: (i,) + (0,) * (len(shape) - 1))


def worth(microseconds):
    return pl.CostEstimate(
        flops=int(microseconds * 1e9), bytes_accessed=1 << 20, transcendentals=0
    )


def params():
    return pltpu.CompilerParams(
        dimension_semantics=("arbitrary",), vmem_limit_bytes=VMEM_BYTES
    )


def attn_forward(state, w_qkv, w_proj, gains, biases, seq_len):
    slots, padded, width = state.shape
    heads = width // HEAD_DIM
    outs = [
        jax.ShapeDtypeStruct((slots, padded, width), jnp.bfloat16),
        jax.ShapeDtypeStruct((slots, padded, 3 * width), jnp.bfloat16),
        jax.ShapeDtypeStruct((slots, heads, padded, padded), jnp.bfloat16),
        jax.ShapeDtypeStruct((slots, padded, width), jnp.bfloat16),
        jax.ShapeDtypeStruct((slots, padded, width), jnp.float32),
    ]
    return pl.pallas_call(
        partial(attn_forward_kernel, seq_len),
        grid=(slots,),
        in_specs=[slot_block(state.shape)]
        + [whole(v.shape) for v in (w_qkv, w_proj, gains, biases)],
        out_specs=[slot_block(o.shape) for o in outs],
        out_shape=outs,
        compiler_params=params(),
        cost_estimate=worth(1),
        name="attn_forward",
    )(state, w_qkv, w_proj, gains, biases)


def mlp_forward_kernel(middle_ref, w_fc1_ref, w_fc2_ref, gains_ref, biases_ref, fc1_bias_ref,
                       normed_ref, hidden_ref, slope_ref, final_ref):
    block = pl.program_id(0)
    slots = middle_ref.shape[0]

    @pl.when(block == 0)
    def _():
        def first(slot, carry):
            middle = middle_ref[slot]
            scaled, _ = norm_parts(middle)
            normed_ref[slot] = (scaled * gains_ref[1:2] + biases_ref[4:5]).astype(jnp.bfloat16)
            final_ref[slot] = middle + biases_ref[5:6]
            return carry

        lax.fori_loop(0, slots, first, 0)

    def rows(slot, carry):
        pre = dot(normed_ref[slot], w_fc1_ref[...], MATMUL_NT) + fc1_bias_ref[0]
        below = 0.5 * (1.0 + lax.erf(pre * 0.5**0.5))
        hidden = (pre * below).astype(jnp.bfloat16)
        bell = jnp.exp(-0.5 * (pre * pre)) * (2.0 * math.pi) ** -0.5
        slope_ref[slot] = (below + pre * bell).astype(jnp.bfloat16)
        hidden_ref[slot] = hidden
        final_ref[slot] += dot(hidden, w_fc2_ref[0], MATMUL_NT)
        return carry

    lax.fori_loop(0, slots, rows, 0)


def mlp_forward(middle, w_fc1, w_fc2, gains, biases, fc1_bias):
    slots, padded, width = middle.shape
    blocks = w_fc2.shape[0]
    wide = (slots, padded, blocks * width)
    outs = [
        jax.ShapeDtypeStruct(middle.shape, jnp.bfloat16),
        jax.ShapeDtypeStruct(wide, jnp.bfloat16),
        jax.ShapeDtypeStruct(wide, jnp.bfloat16),
        jax.ShapeDtypeStruct(middle.shape, jnp.float32),
    ]
    wide_spec = pl.BlockSpec((slots, padded, width), lambda i: (0, 0, i))
    return pl.pallas_call(
        mlp_forward_kernel,
        grid=(blocks,),
        in_specs=[
            whole(middle.shape),
            pl.BlockSpec((width, width), lambda i: (i, 0)),
            pl.BlockSpec((1, width, width), lambda i: (i, 0, 0)),
            whole(gains.shape),
            whole(biases.shape),
            pl.BlockSpec((1, 1, width), lambda i: (i, 0, 0)),
        ],
        out_specs=[whole(middle.shape), wide_spec, wide_spec, whole(middle.shape)],
        out_shape=outs,
        compiler_params=params(),
        cost_estimate=worth(1),
        name="mlp_forward",
    )(middle, w_fc1, w_fc2, gains, biases, fc1_bias)


def mlp_backward_kernel(mode, cut, me_ref, grad_ref, middle_ref, normed_ref, hidden_ref, slope_ref, w_fc1_ref,
                        w_fc2_ref, gains_ref, *refs):
    share_count = 1 if mode == "joined" else 2
    share_refs = refs[:share_count]
    fc1_sums_ref, sums_ref, out_ref, branch_ref, pre_ref, total_ref, before_ref = refs[share_count:]
    block = pl.program_id(0)
    slots, padded, width = grad_ref.shape

    @pl.when(block == 0)
    def _():
        sums_ref[...] = jnp.zeros_like(sums_ref)

        def first(slot, carry):
            branch = grad_ref[slot].astype(jnp.bfloat16)
            branch_ref[pl.ds(pl.multiple_of(slot * padded, TILE_ROWS), padded), :] = branch
            sums_ref[2:3] += column_sums(branch)
            return carry

        lax.fori_loop(0, slots, first, 0)

    fc1_sums_ref[...] = jnp.zeros_like(fc1_sums_ref)

    def rows(slot, carry):
        here = pl.ds(pl.multiple_of(slot * padded, TILE_ROWS), padded)
        grad_hidden = dot(branch_ref[here, :], w_fc2_ref[0], MATMUL_NN)
        grad_pre = (grad_hidden * slope_ref[slot].astype(jnp.float32)).astype(jnp.bfloat16)
        pre_ref[here, :] = grad_pre
        fc1_sums_ref[0, 0:1] += column_sums(grad_pre)
        part = dot(grad_pre, w_fc1_ref[...], MATMUL_NN)

        @pl.when(block == 0)
        def _():
            total_ref[slot] = part

        @pl.when(block != 0)
        def _():
            total_ref[slot] += part

        return carry

    lax.fori_loop(0, slots, rows, 0)
    hidden = hidden_ref[...].reshape(slots * padded, width)
    normed = normed_ref[...].reshape(slots * padded, width)
    if mode == "plain":
        grad_fc1_ref, grad_fc2_ref = share_refs
        step = 2 * LANES
        for at in range(0, width, step):
            grad_fc2_ref[0, at : at + step, :] = dot(
                branch_ref[:, at : at + step], hidden, MATMUL_TN
            ).astype(jnp.bfloat16)
            grad_fc1_ref[at : at + step, :] = dot(
                pre_ref[:, at : at + step], normed, MATMUL_TN
            ).astype(jnp.bfloat16)
    else:
        tall = 4 * cut
        for at in range(0, width, SHARE_STEP):
            value = dot(pre_ref[:, at : at + SHARE_STEP], normed, MATMUL_TN)
            value = value.reshape(SHARE_STEP // tall, tall, width)
            for s in range(0, SHARE_STEP // tall, 2):
                pair = block * (width // tall // 2) + at // tall // 2 + s // 2
                put(share_refs, me_ref, pair, slice(0, tall), value[s], value[s + 1])
            value = dot(branch_ref[:, at : at + SHARE_STEP], hidden, MATMUL_TN)

            @pl.when(block % 2 == 0)
            def _():
                before_ref[at : at + SHARE_STEP, :] = value

            for odd in range(1, 4, 2):

                @pl.when(block == odd)
                def _():
                    before = before_ref[at : at + SHARE_STEP, :].reshape(-1, cut, width)
                    both = jnp.concatenate([before, value.reshape(-1, cut, width)], 1)
                    rows = slice(tall + (odd - 1) * cut, tall + (odd + 1) * cut)
                    for s in range(0, SHARE_STEP // cut, 2):
                        pair = at // cut // 2 + s // 2
                        put(share_refs, me_ref, pair, rows, both[s], both[s + 1])

    @pl.when(block == pl.num_programs(0) - 1)
    def _():
        def last(slot, carry):
            grad_normed = total_ref[slot]
            scaled, inv_std = norm_parts(middle_ref[slot])
            sums_ref[0:1] += column_sums(grad_normed * scaled)
            sums_ref[1:2] += column_sums(grad_normed)
            out_ref[slot] = grad_ref[slot] + norm_back(
                grad_normed, scaled, inv_std, gains_ref[1:2]
            )
            return carry

        lax.fori_loop(0, slots, last, 0)


def mlp_backward(mode, devices, me, grad, middle, normed, hidden, slope, w_fc1, w_fc2, gains):
    slots, padded, width = grad.shape
    blocks = w_fc2.shape[0]
    cut = width // devices
    fc1_spec = pl.BlockSpec((width, width), lambda i: (i, 0))
    fc2_spec = pl.BlockSpec((1, width, width), lambda i: (i, 0, 0))
    if mode == "plain":
        shares = [jax.ShapeDtypeStruct(v.shape, jnp.bfloat16) for v in (w_fc1, w_fc2)]
        share_specs = [fc1_spec, fc2_spec]
    else:
        shares = share_shapes(mode, devices, 8 * cut, width)
        share_specs = [whole(v.shape) for v in shares]
    outs = shares + [
        jax.ShapeDtypeStruct((blocks, 8, width), jnp.float32),
        jax.ShapeDtypeStruct((8, width), jnp.float32),
        jax.ShapeDtypeStruct(grad.shape, jnp.float32),
    ]
    wide_spec = pl.BlockSpec((slots, padded, width), lambda i: (0, 0, i))
    return pl.pallas_call(
        partial(mlp_backward_kernel, mode, cut),
        grid=(blocks,),
        in_specs=[pl.BlockSpec(memory_space=pltpu.SMEM)]
        + [whole(grad.shape), whole(grad.shape), whole(grad.shape)]
        + [wide_spec, wide_spec, fc1_spec, fc2_spec, whole(gains.shape)],
        out_specs=share_specs
        + [
            pl.BlockSpec((1, 8, width), lambda i: (i, 0, 0)),
            whole((8, width)),
            whole(grad.shape),
        ],
        out_shape=outs,
        scratch_shapes=[
            pltpu.VMEM((slots * padded, width), jnp.bfloat16),
            pltpu.VMEM((slots * padded, width), jnp.bfloat16),
            pltpu.VMEM(grad.shape, jnp.float32),
            pltpu.VMEM((width, width), jnp.float32),
        ],
        compiler_params=params(),
        cost_estimate=worth(BACKWARD_WORTH),
        name="mlp_backward",
    )(me, grad, middle, normed, hidden, slope, w_fc1, w_fc2, gains)


def attn_backward_kernel(mode, cut, me_ref, grad_ref, x_ref, normed_ref, mixed_ref, probs_ref, attended_ref,
                         w_qkv_ref, w_proj_ref, gains_ref, *refs):
    share_count = 1 if mode == "joined" else 2
    share_refs = refs[:share_count]
    sums_ref, out_ref, mixed_all, normed_all, attended_all, branch_all = refs[share_count:]
    slot = pl.program_id(0)
    _, padded, width = grad_ref.shape
    here = pl.ds(pl.multiple_of(slot * padded, TILE_ROWS), padded)

    @pl.when(slot == 0)
    def _():
        sums_ref[...] = jnp.zeros_like(sums_ref)

    branch = grad_ref[0].astype(jnp.bfloat16)
    branch_all[here, :] = branch
    normed_all[here, :] = normed_ref[0]
    attended_all[here, :] = attended_ref[0]
    grad_attended = dot(branch, w_proj_ref[...], MATMUL_NN).astype(jnp.bfloat16)
    for pair in range(width // LANES):
        at = pair * LANES
        query = mixed_ref[0, :, at : at + LANES]
        key = mixed_ref[0, :, width + at : width + at + LANES]
        value = mixed_ref[0, :, 2 * width + at : 2 * width + at + LANES]
        grad_pair = grad_attended[:, at : at + LANES]
        grad_query = grad_key = grad_value = 0.0
        for side in range(2):
            probs = probs_ref[0, 2 * pair + side]
            wide_probs = probs.astype(jnp.float32)
            grad_side = side_of(grad_pair, side)
            grad_value += dot(probs, grad_side, MATMUL_TN)
            grad_probs = dot(grad_side, value, MATMUL_NT)
            row_inner = jnp.sum(grad_probs * wide_probs, -1, keepdims=True)
            grad_scores = (wide_probs * (grad_probs - row_inner)).astype(jnp.bfloat16)
            grad_query += dot(grad_scores, side_of(key, side), MATMUL_NN)
            grad_key += dot(grad_scores, side_of(query, side), MATMUL_TN)
        grad_query = (grad_query * HEAD_DIM ** (-0.5)).astype(jnp.bfloat16)
        mixed_all[here, at : at + LANES] = grad_query
        mixed_all[here, width + at : width + at + LANES] = grad_key.astype(jnp.bfloat16)
        mixed_all[here, 2 * width + at : 2 * width + at + LANES] = grad_value.astype(jnp.bfloat16)
    grad_mixed = mixed_all[here, :]
    sums_ref[2:3] += column_sums(grad_mixed[:, :width])
    sums_ref[3:4] += column_sums(grad_mixed[:, 2 * width :])
    sums_ref[4:5] += column_sums(branch)
    grad_normed = dot(grad_mixed, w_qkv_ref[...], MATMUL_NN)
    scaled, inv_std = norm_parts(x_ref[0])
    sums_ref[0:1] += column_sums(grad_normed * scaled)
    sums_ref[1:2] += column_sums(grad_normed)
    out_ref[0] = grad_ref[0] + norm_back(grad_normed, scaled, inv_std, gains_ref[0:1])

    @pl.when(slot == pl.num_programs(0) - 1)
    def _():
        if mode == "plain":
            grad_qkv_ref, grad_proj_ref = share_refs
            step = 2 * LANES
            for at in range(0, 3 * width, step):
                grad_qkv_ref[at : at + step, :] = dot(
                    mixed_all[:, at : at + step], normed_all[...], MATMUL_TN
                ).astype(jnp.bfloat16)
            for at in range(0, width, step):
                grad_proj_ref[at : at + step, :] = dot(
                    branch_all[:, at : at + step], attended_all[...], MATMUL_TN
                ).astype(jnp.bfloat16)
        else:
            for at in range(0, width, SHARE_STEP):
                three = slice(3 * at, 3 * (at + SHARE_STEP))
                value = dot(mixed_all[:, three], normed_all[...], MATMUL_TN)
                more = dot(
                    branch_all[:, at : at + SHARE_STEP], attended_all[...], MATMUL_TN
                )
                both = jnp.concatenate(
                    [value.reshape(-1, 3 * cut, width), more.reshape(-1, cut, width)], 1
                )
                for s in range(0, SHARE_STEP // cut, 2):
                    pair = at // cut // 2 + s // 2
                    put(share_refs, me_ref, pair, slice(0, 4 * cut), both[s], both[s + 1])


def attn_backward(mode, devices, me, grad, state, normed, mixed, probs, attended, w_qkv, w_proj, gains, length):
    slots, padded, width = grad.shape
    cut = width // devices
    if mode == "plain":
        shares = [jax.ShapeDtypeStruct(v.shape, jnp.bfloat16) for v in (w_qkv, w_proj)]
    else:
        shares = share_shapes(mode, devices, 4 * cut + TILE_ROWS, width)
    outs = shares + [
        jax.ShapeDtypeStruct((8, width), jnp.float32),
        jax.ShapeDtypeStruct(grad.shape, jnp.float32),
    ]
    sliced = (grad, state, normed, mixed, probs, attended)
    return pl.pallas_call(
        partial(attn_backward_kernel, mode, cut),
        grid=(slots,),
        in_specs=[pl.BlockSpec(memory_space=pltpu.SMEM)]
        + [slot_block(v.shape) for v in sliced]
        + [whole(v.shape) for v in (w_qkv, w_proj, gains)],
        out_specs=[whole(o.shape) for o in outs[:-1]] + [slot_block(grad.shape)],
        out_shape=outs,
        scratch_shapes=[
            pltpu.VMEM((slots * padded, 3 * width), jnp.bfloat16),
            pltpu.VMEM((slots * padded, width), jnp.bfloat16),
            pltpu.VMEM((slots * padded, width), jnp.bfloat16),
            pltpu.VMEM((slots * padded, width), jnp.bfloat16),
        ],
        compiler_params=params(),
        cost_estimate=worth(length),
        name="attn_backward",
    )(me, *sliced, w_qkv, w_proj, gains)


def spread(share, place, refs):
    at = 0
    for ref in refs:
        rows = ref.shape[-2]
        for block in range(ref.shape[0]) if len(ref.shape) == 4 else [None]:
            piece = share[at : at + rows].astype(jnp.bfloat16)
            at += rows
            if block is None:
                ref[place] = piece
            else:
                ref[block, place] = piece


def unpack_kernel(blob_ref, *refs):
    for i in range(blob_ref.shape[0]):
        spread(blob_ref[i].astype(jnp.float32), i, refs)


def unpack_relative_kernel(count, me_ref, *refs):
    chips = pl.num_programs(0)
    for i in range(count):
        place = 2 * chips * (i // 2) + 2 * pl.program_id(0) + i % 2
        spread(refs[i][0].astype(jnp.float32), place ^ me_ref[0], refs[count:])


def unpack_whole(blob, shapes):
    devices, rows, width = blob.shape
    step = 4
    specs = [
        pl.BlockSpec((step, *s[1:]), lambda i: (i, 0, 0))
        if len(s) == 3
        else pl.BlockSpec((s[0], step, *s[2:]), lambda i: (0, i, 0, 0))
        for s in shapes
    ]
    return pl.pallas_call(
        unpack_kernel,
        grid=(devices // step,),
        in_specs=[pl.BlockSpec((step, rows, width), lambda i: (i, 0, 0))],
        out_specs=specs,
        out_shape=[jax.ShapeDtypeStruct(s, jnp.bfloat16) for s in shapes],
        compiler_params=params(),
        cost_estimate=worth(1),
        name="unpack_whole",
    )(blob)


def unpack_relative(pieces, me, shapes):
    return pl.pallas_call(
        partial(unpack_relative_kernel, len(pieces)),
        grid=(pieces[0].shape[0],),
        in_specs=[pl.BlockSpec(memory_space=pltpu.SMEM)] + [slot_block(p.shape) for p in pieces],
        out_specs=[whole(s) for s in shapes],
        out_shape=[jax.ShapeDtypeStruct(s, jnp.bfloat16) for s in shapes],
        compiler_params=params(),
        cost_estimate=worth(1),
        name="unpack_relative",
    )(me, *pieces)


AXES = ("dp", "fsdp")


def pack_layer(w_qkv, w_proj, w_fc1, w_fc2, gains, biases, fc1_bias):
    width, tall = w_qkv.shape[0], w_fc2.shape[0]
    cut = w_fc2.T.reshape(w_fc2.shape[1], tall // width, width).transpose(1, 0, 2)
    small = jnp.concatenate([gains.reshape(-1), biases.reshape(-1), fc1_bias.reshape(-1)])
    small = jnp.pad(small, (0, -small.size % width)).reshape(-1, width)
    small = jnp.pad(small, ((0, -small.shape[0] % 16), (0, 0)))
    return jnp.concatenate([w_qkv.T, w_proj.T, w_fc1.T, cut.reshape(-1, width), small], 0)


def unpack_layer(blob, shapes):
    devices, _, width = blob.shape
    qkv, proj, fc1, fc2, gains, biases, fc1_bias = shapes
    at = 0
    parts = []
    for columns in (qkv[1], proj[1], fc1[1]):
        parts.append(blob[:, at : at + columns].reshape(-1, width))
        at += columns
    blocks = fc2[0] // width
    cut = blob[:, at : at + blocks * fc2[1]].reshape(devices, blocks, fc2[1], width)
    parts.append(cut.transpose(1, 0, 2, 3).reshape(blocks, devices * fc2[1], width))
    at += blocks * fc2[1]
    small = unpack_small(blob[:, at:], (gains, biases, fc1_bias))
    small[2] = small[2].reshape(blocks, 1, width)
    return tuple(parts) + tuple(small)


def unpack_small(small, shapes):
    devices = small.shape[0]
    small = small.reshape(devices, -1)
    parts, start = [], 0
    for rows, columns in shapes:
        piece = small[:, start : start + rows * columns].reshape(devices, rows, columns)
        piece = piece.transpose(1, 0, 2).astype(jnp.float32)
        parts.append(piece.reshape(rows, devices * columns))
        start += rows * columns
    return parts


def pack_grads(grads, shapes, total_rows, devices):
    grad_qkv, grad_proj, grad_fc1, grad_fc2, gains_grad, biases_grad, fc1_grad = grads
    width = grad_qkv.shape[1]
    qkv, proj, fc1, fc2, gains, biases, fc1_bias = shapes
    blob = jnp.zeros((devices, total_rows, width), jnp.bfloat16)
    at = 0
    for value in (grad_qkv, grad_proj, grad_fc1):
        rows = value.shape[0] // devices
        blob = blob.at[:, at : at + rows].set(
            value.astype(jnp.bfloat16).reshape(devices, rows, width)
        )
        at += rows
    blocks = fc2[0] // width
    cut = grad_fc2.reshape(blocks, devices, fc2[1], width).transpose(1, 0, 2, 3)
    blob = blob.at[:, at : at + blocks * fc2[1]].set(cut.reshape(devices, -1, width))
    at += blocks * fc2[1]
    small = []
    for value, (rows, columns) in ((gains_grad, gains), (biases_grad, biases), (fc1_grad, fc1_bias)):
        small.append(value.reshape(rows, devices, columns).transpose(1, 0, 2).reshape(devices, -1))
    small = jnp.concatenate(small, 1).astype(jnp.bfloat16)
    small = jnp.pad(small, ((0, 0), (0, -small.shape[1] % width))).reshape(devices, -1, width)
    return blob.at[:, at : at + small.shape[1]].set(small)


def unpack_grads(blob, shapes):
    width = blob.shape[1]
    qkv, proj, fc1, fc2, gains, biases, fc1_bias = shapes
    blob = blob.astype(jnp.float32)
    at = 0
    parts = []
    for columns in (qkv[1], proj[1], fc1[1]):
        parts.append(blob[at : at + columns].T)
        at += columns
    blocks = fc2[0] // width
    cut = blob[at : at + blocks * fc2[1]].reshape(blocks, fc2[1], width)
    parts.append(cut.transpose(0, 2, 1).reshape(fc2))
    at += blocks * fc2[1]
    small = blob[at:].reshape(-1)
    start = 0
    for rows, columns in (gains, biases, fc1_bias):
        parts.append(small[start : start + rows * columns].reshape(rows, columns))
        start += rows * columns
    return tuple(parts)


def small_shares(values, devices):
    cut = [v.reshape(v.shape[0], devices, -1).transpose(1, 0, 2) for v in values]
    return jnp.concatenate([v.reshape(devices, -1) for v in cut], 1).astype(jnp.bfloat16)


def small_rows(row, width):
    row = jnp.pad(row, ((0, 0), (0, -row.shape[1] % (TILE_ROWS * width))))
    return row.reshape(row.shape[0], -1, width)


def swap(value, axis, mask, size):
    return lax.ppermute(value, axis, [(i, i ^ mask) for i in range(size)])


def total_of(values):
    return sum(v.astype(jnp.float32) for v in values).astype(jnp.bfloat16)


class Exchange:
    def __init__(self, mine, other, fsdp_size, orders):
        rows, width = mine.shape[-2:]
        self.fsdp_size = fsdp_size
        self.orders = [list(order) for order in orders]
        self.kept = mine
        self.shape = (2, 2, fsdp_size // 2, rows // len(orders), width)
        self.pending = None if other is None else [[swap(other, "fsdp", 1, fsdp_size)]]

    def sums(self):
        if self.pending is None:
            return [self.kept]
        if isinstance(self.kept, list):
            return [total_of([k, *got]) for k, got in zip(self.kept, self.pending)]
        got = self.pending[0][0]
        rows = self.shape[3]
        cuts = [slice(i * rows, (i + 1) * rows) for i in range(len(self.orders))]
        return [total_of([self.kept[:, c], got[:, c]]).reshape(self.shape) for c in cuts]

    def step(self):
        kept, pending = [], []
        for value, order in zip(self.sums(), self.orders):
            stage = order.pop(0)
            if stage == "z":
                kept.append(value[:, :, :1])
                pending.append(
                    [
                        swap(value[:, :, i : i + 1], "fsdp", 2 * i, self.fsdp_size)
                        for i in range(1, self.fsdp_size // 2)
                    ]
                )
            elif stage == "x":
                kept.append(value[:, :1])
                pending.append([swap(value[:, 1:], "dp", 1, 4)])
            elif stage == "y":
                kept.append(value[:1])
                pending.append([swap(value[1:], "dp", 2, 4)])
            else:
                kept.append(value[:1, :1])
                pending.append(
                    [
                        swap(value[i // 2 : i // 2 + 1, i % 2 : i % 2 + 1], "dp", i, 4)
                        for i in range(1, 4)
                    ]
                )
        self.kept, self.pending = kept, pending

    def result(self):
        return jnp.concatenate([v.reshape(self.shape[3:]) for v in self.sums()], 0)


def gate(values, *exchanges):
    values, arrived = lax.optimization_barrier((values, [e.pending for e in exchanges]))
    for exchange, pending in zip(exchanges, arrived):
        exchange.pending = pending
    return values


HALVES = (("x", "y"), ("y", "x"))
WHOLE = (("xy", "z"),)


def on_device(dp_size, fsdp_size, images, counts, cotangent, *weights):
    slots, seq_len, width = images.shape
    layer_count = weights[0].shape[0]
    shapes = [w.shape[1:] for w in weights]
    devices = dp_size * fsdp_size
    cut = width // devices
    direct = dp_size == 4 and layer_count == 2 and cut % 8 == 0 and SHARE_STEP % (8 * cut) == 0 and devices * cut == width
    live = (jnp.arange(slots) < counts[0]).astype(jnp.float32)[:, None, None]
    me = lax.axis_index("dp") * fsdp_size + lax.axis_index("fsdp")
    place = jnp.arange(devices)
    place = (jnp.bitwise_xor(2 * (place % (devices // 2)) + place // (devices // 2), me))[:, None]
    relative = (place == jnp.arange(devices)[None]).astype(jnp.bfloat16)
    me = me.astype(jnp.int32).reshape(1)
    extra = ((0, 0), (0, -seq_len % TILE_ROWS), (0, 0))
    state = jnp.pad(images.astype(jnp.float32), extra)
    blocks = shapes[3][0] // width
    every = [(layer_count * n, m) for n, m in shapes[4:]]
    share_rows = -(-sum(n * m for n, m in every) // width)
    share_rows = -(-share_rows // TILE_ROWS) * TILE_ROWS
    ahead = [(devices, 3 * cut, width), (devices, cut, width)]
    behind = [(devices, 4 * cut, width), (blocks, devices, cut, width)]
    little = [(devices, share_rows, width)]

    def attn_of(layer_index, state):
        w_qkv, w_proj, _, _, gains, biases, _ = gathered[layer_index]
        return (state, *attn_forward(state, w_qkv, w_proj, gains, biases, seq_len))

    def mlp_of(layer_index, middle):
        _, _, w_fc1, w_fc2, gains, biases, fc1_bias = gathered[layer_index]
        return mlp_forward(middle, w_fc1, w_fc2, gains, biases, fc1_bias)

    shares = [pack_layer(*(w[i] for w in weights)) for i in range(layer_count)]
    share = shares[0]
    if direct:
        row = jnp.concatenate([w.reshape(1, -1) for w in weights[4:]], 1)
        row = jnp.pad(row, ((0, 0), (0, share_rows * width - row.shape[1])))
        share = jnp.concatenate([share[: 12 * cut], row.reshape(-1, width)], 0)
        blob = lax.all_gather(share, AXES, axis=0, tiled=False)
        late = shares[1][4 * cut : 12 * cut]
        blob_one = lax.all_gather(shares[1][: 4 * cut], AXES, axis=0, tiled=False)
        blob, late = lax.optimization_barrier((blob, late))
        rows = [late] + [swap(late, "fsdp", 2 * i, fsdp_size) for i in range(1, fsdp_size // 2)]
        *parts, small = unpack_whole(blob, ahead + behind + little)
        parts = [v.reshape(-1, width) for v in parts[:3]] + [parts[3].reshape(blocks, -1, width)]
        little_all = unpack_small(small, every)
        little_of = [
            [v[i * n : (i + 1) * n] for v, (n, _) in zip(little_all, shapes[4:])]
            for i in range(layer_count)
        ]
        for i in range(layer_count):
            little_of[i][2] = little_of[i][2].reshape(blocks, 1, width)
        parts, little_of = lax.optimization_barrier((parts, little_of))
        gathered = [(*parts, *little_of[0]), None]
        *saved, middle = attn_of(0, state)
        middle, rows = lax.optimization_barrier((middle, rows))
        rows = jnp.stack(rows)
        near = [rows] + [swap(rows, "dp", i, dp_size) for i in range(1, dp_size)]
        *more, final = mlp_of(0, middle)
        kept = [(*saved, middle, *more)]
        blob_one, final = lax.optimization_barrier((blob_one, final))
        w_qkv, w_proj = unpack_whole(blob_one, ahead)
        w_qkv, near = lax.optimization_barrier((w_qkv, near))
        pieces = [v for n in near for v in (n, swap(n, "fsdp", 1, fsdp_size))]
        w_qkv, w_proj = w_qkv.reshape(-1, width), w_proj.reshape(-1, width)
        gathered[1] = (w_qkv, w_proj, None, None, *little_of[1])
        *saved, middle = attn_of(1, final)
        middle, pieces = lax.optimization_barrier((middle, pieces))
        w_fc1, w_fc2 = unpack_relative(pieces, me, behind)
        w_fc1, w_fc2 = w_fc1.reshape(-1, width), w_fc2.reshape(blocks, -1, width)
        gathered[1] = (w_qkv, w_proj, w_fc1, w_fc2, *gathered[1][4:])
        *more, state = mlp_of(1, middle)
        kept.append((*saved, middle, *more))
    else:
        gathered = [lax.all_gather(v, AXES, axis=0, tiled=False) for v in shares]
        kept = []
        for layer_index in range(layer_count):
            blob, state = lax.optimization_barrier((gathered[layer_index], state))
            gathered[layer_index] = unpack_layer(blob, shapes)
            *saved, middle = attn_of(layer_index, state)
            *more, state = mlp_of(layer_index, middle)
            kept.append((*saved, middle, *more))
    block_output = (state[:, :seq_len] * live).astype(jnp.bfloat16)
    grad_state = jnp.pad(cotangent.astype(jnp.float32) * live, extra)
    layer_grads = [None] * layer_count

    def small_of(mlp, attn):
        fc1_sums, mlp_sums = mlp
        gains_grad = jnp.stack([attn[0], mlp_sums[0]])
        biases_grad = jnp.stack([attn[1], attn[2], attn[3], attn[4], mlp_sums[1], mlp_sums[2]])
        return (gains_grad, biases_grad, fc1_sums[:, 0].reshape(1, -1))

    def mlp_part(layer_index, mode, grad_state):
        w_fc1, w_fc2, gains = gathered[layer_index][2:5]
        middle, normed, hidden, slope = kept[layer_index][5:]
        *shares, fc1_sums, sums, grad_middle = mlp_backward(
            mode, devices, me, grad_state, middle, normed, hidden, slope, w_fc1, w_fc2, gains
        )
        return shares, (fc1_sums, sums), grad_middle

    def attn_part(layer_index, mode, grad_middle):
        w_qkv, w_proj, gains = (gathered[layer_index][i] for i in (0, 1, 4))
        *shares, sums, grad_state = attn_backward(
            mode, devices, me, grad_middle, *kept[layer_index][:5], w_qkv, w_proj, gains,
            1 if layer_index else 200
        )
        return shares, sums, grad_state

    def with_small(shares, mlp, attn):
        row = small_shares(small_of(mlp, attn), devices)
        row = jnp.dot(relative, row, preferred_element_type=jnp.float32).astype(jnp.bfloat16)
        row = small_rows(row, width)
        count = shares[0].shape[0]
        return [v.at[:, 4 * cut :].set(row[i * count : (i + 1) * count]) for i, v in enumerate(shares)]

    def owned(attn_sum, mlp_sum):
        summed = jnp.concatenate([attn_sum[: 4 * cut], mlp_sum, attn_sum[4 * cut :]], 0)
        return unpack_grads(summed, shapes)

    if direct:
        shares, mlp, grad_middle = mlp_part(1, "split", grad_state)
        mlp_one = Exchange(*shares, fsdp_size, HALVES)
        shares, attn, grad_state = attn_part(1, "split", grad_middle)
        shares, attn, grad_state = gate((shares, attn, grad_state), mlp_one)
        mlp_one.step()
        attn_one = Exchange(*with_small(shares, mlp, attn), fsdp_size, WHOLE)
        shares, mlp, grad_middle = mlp_part(0, "joined", grad_state)
        mlp_zero = lax.psum_scatter(shares[0], AXES, scatter_dimension=0, tiled=False)
        grad_middle, mlp = gate((grad_middle, mlp), mlp_one, attn_one)
        mlp_one.step()
        attn_one.step()
        shares, attn, grad_state = attn_part(0, "split", grad_middle)
        shares, attn, grad_state = gate((shares, attn, grad_state), mlp_one, attn_one)
        late = mlp_one.sums() + attn_one.sums()
        late = Exchange(jnp.concatenate(late, 3), None, fsdp_size, (("z",),))
        late.step()
        attn_zero = Exchange(*with_small(shares, mlp, attn), fsdp_size, WHOLE)
        attn_zero.step()
        arrived = attn_zero.pending
        late.pending, arrived = lax.optimization_barrier((late.pending, arrived))
        attn_zero.step()
        late = late.result()
        layer_grads[1] = owned(late[8 * cut :], late[: 8 * cut])
        layer_grads[0] = owned(attn_zero.result(), mlp_zero)
    else:
        for layer_index in reversed(range(layer_count)):
            mlp_shares, mlp, grad_middle = mlp_part(layer_index, "plain", grad_state)
            attn_shares, attn, grad_state = attn_part(layer_index, "plain", grad_middle)
            grads = (*attn_shares, *mlp_shares, *small_of(mlp, attn))
            packed = pack_grads(grads, shapes, share.shape[0], devices)
            summed = lax.psum_scatter(packed, AXES, scatter_dimension=0, tiled=False)
            layer_grads[layer_index] = unpack_grads(summed, shapes)
    stacked = tuple((jnp.stack([entry[member] for entry in layer_grads]) for member in range(7)))
    return (block_output, grad_state[:, :seq_len], *stacked)


def solution(mesh):
    placed = (
        P(("dp", "fsdp"), None, None),
        P(("dp", "fsdp")),
        P(("dp", "fsdp"), None, None),
        P(None, None, ("dp", "fsdp")),
        P(None, None, ("dp", "fsdp")),
        P(None, None, ("dp", "fsdp")),
        P(None, None, ("dp", "fsdp")),
        P(None, None, ("dp", "fsdp")),
        P(None, None, ("dp", "fsdp")),
        P(None, None, ("dp", "fsdp")),
    )
    return jax.shard_map(
        partial(on_device, mesh.shape["dp"], mesh.shape["fsdp"]),
        mesh=mesh,
        in_specs=placed,
        out_specs=(
            P(("dp", "fsdp"), None, None),
            P(("dp", "fsdp"), None, None),
            P(None, None, ("dp", "fsdp")),
            P(None, None, ("dp", "fsdp")),
            P(None, None, ("dp", "fsdp")),
            P(None, None, ("dp", "fsdp")),
            P(None, None, ("dp", "fsdp")),
            P(None, None, ("dp", "fsdp")),
            P(None, None, ("dp", "fsdp")),
        ),
        check_vma=False,
    )
```

```python
import math
from functools import partial

import jax
import jax.numpy as jnp
from jax import lax
from jax.experimental import pallas as pl
from jax.experimental.pallas import tpu as pltpu
from jax.sharding import PartitionSpec as P

HEAD_DIM = 64
MATMUL_NT = (((1,), (1,)), ((), ()))
MATMUL_NN = (((1,), (0,)), ((), ()))
MATMUL_TN = (((0,), (0,)), ((), ()))
VMEM_BYTES = 60 * 1024 * 1024
TILE_ROWS = 16
LANES = 128
SHARE_STEP = 384
BACKWARD_WORTH = 1
MASKED = -1e30


def dot(left, right, dims):
    return lax.dot_general(left, right, dims, preferred_element_type=jnp.float32)


def norm_parts(token_rows):
    row_mean = jnp.mean(token_rows, -1, keepdims=True)
    centered = token_rows - row_mean
    inv_std = lax.rsqrt(jnp.mean(centered * centered, -1, keepdims=True) + 1e-06)
    return (centered * inv_std, inv_std)


def norm_back(grad_normed, scaled, inv_std, gain_row):
    grad_scaled = grad_normed * gain_row
    return inv_std * (
        grad_scaled
        - jnp.mean(grad_scaled, -1, keepdims=True)
        - scaled * jnp.mean(grad_scaled * scaled, -1, keepdims=True)
    )


def column_sums(rows):
    return jnp.sum(rows.astype(jnp.float32), 0, keepdims=True)


def side_of(pair, side):
    lane = lax.broadcasted_iota(jnp.int32, pair.shape, 1)
    mine = (lane >= HEAD_DIM) if side else (lane < HEAD_DIM)
    return jnp.where(mine, pair, jnp.zeros_like(pair))


def put(refs, me_ref, pair, rows, even, odd):
    if len(refs) == 1:
        refs[0][2 * pair, rows, :] = even.astype(jnp.bfloat16)
        refs[0][2 * pair + 1, rows, :] = odd.astype(jnp.bfloat16)
    else:
        place = pair ^ (me_ref[0] >> 1)
        low = (me_ref[0] & 1) == 0
        refs[0][place, rows, :] = jnp.where(low, even, odd).astype(jnp.bfloat16)
        refs[1][place, rows, :] = jnp.where(low, odd, even).astype(jnp.bfloat16)


def share_shapes(mode, devices, rows, width):
    if mode == "joined":
        return [jax.ShapeDtypeStruct((devices, rows, width), jnp.bfloat16)]
    return [jax.ShapeDtypeStruct((devices // 2, rows, width), jnp.bfloat16)] * 2


def attn_forward_kernel(seq_len, x_ref, w_qkv_ref, w_proj_ref, gains_ref, biases_ref,
                        normed_ref, mixed_ref, probs_ref, attended_ref, middle_ref):
    width = x_ref.shape[2]
    token_rows = x_ref[0]
    scaled, _ = norm_parts(token_rows)
    normed = (scaled * gains_ref[0:1] + biases_ref[0:1]).astype(jnp.bfloat16)
    normed_ref[0] = normed
    for part in range(3):
        columns = slice(part * width, (part + 1) * width)
        mixed = dot(normed, w_qkv_ref[columns, :], MATMUL_NT)
        if part == 0:
            mixed = mixed + biases_ref[1:2]
        if part == 2:
            mixed = mixed + biases_ref[2:3]
        mixed = mixed.astype(jnp.bfloat16)
        if part == 0:
            mixed = mixed * jnp.bfloat16(HEAD_DIM ** (-0.5))
        mixed_ref[0, :, columns] = mixed
    padded = x_ref.shape[1]
    real_key = lax.broadcasted_iota(jnp.int32, (padded, padded), 1) < seq_len
    for pair in range(width // LANES):
        at = pair * LANES
        query = mixed_ref[0, :, at : at + LANES]
        key = mixed_ref[0, :, width + at : width + at + LANES]
        value = mixed_ref[0, :, 2 * width + at : 2 * width + at + LANES]
        total = None
        for side in range(2):
            scores = dot(side_of(query, side), key, MATMUL_NT)
            scores = jnp.where(real_key, scores, MASKED)
            top = jnp.max(scores, -1, keepdims=True)
            expo = jnp.exp(scores - top)
            probs = (expo / jnp.sum(expo, -1, keepdims=True)).astype(jnp.bfloat16)
            probs_ref[0, 2 * pair + side] = probs
            part = dot(probs, side_of(value, side), MATMUL_NN)
            total = part if total is None else total + part
        attended_ref[0, :, at : at + LANES] = total.astype(jnp.bfloat16)
    middle_ref[0] = (
        token_rows + dot(attended_ref[0], w_proj_ref[...], MATMUL_NT) + biases_ref[3:4]
    )


def whole(shape):
    return pl.BlockSpec(shape, lambda i: (0,) * len(shape), pipeline_mode=pl.Buffered(1))


def slot_block(shape):
    return pl.BlockSpec((1, *shape[1:]), lambda i: (i,) + (0,) * (len(shape) - 1))


def worth(microseconds):
    return pl.CostEstimate(
        flops=int(microseconds * 1e9), bytes_accessed=1 << 20, transcendentals=0
    )


def params():
    return pltpu.CompilerParams(
        dimension_semantics=("arbitrary",), vmem_limit_bytes=VMEM_BYTES
    )


def attn_forward(state, w_qkv, w_proj, gains, biases, seq_len):
    slots, padded, width = state.shape
    heads = width // HEAD_DIM
    outs = [
        jax.ShapeDtypeStruct((slots, padded, width), jnp.bfloat16),
        jax.ShapeDtypeStruct((slots, padded, 3 * width), jnp.bfloat16),
        jax.ShapeDtypeStruct((slots, heads, padded, padded), jnp.bfloat16),
        jax.ShapeDtypeStruct((slots, padded, width), jnp.bfloat16),
        jax.ShapeDtypeStruct((slots, padded, width), jnp.float32),
    ]
    return pl.pallas_call(
        partial(attn_forward_kernel, seq_len),
        grid=(slots,),
        in_specs=[slot_block(state.shape)]
        + [whole(v.shape) for v in (w_qkv, w_proj, gains, biases)],
        out_specs=[slot_block(o.shape) for o in outs],
        out_shape=outs,
        compiler_params=params(),
        cost_estimate=worth(1),
        name="attn_forward",
    )(state, w_qkv, w_proj, gains, biases)


def mlp_forward_kernel(middle_ref, w_fc1_ref, w_fc2_ref, gains_ref, biases_ref, fc1_bias_ref,
                       normed_ref, hidden_ref, slope_ref, final_ref):
    block = pl.program_id(0)
    slots = middle_ref.shape[0]

    @pl.when(block == 0)
    def _():
        def first(slot, carry):
            middle = middle_ref[slot]
            scaled, _ = norm_parts(middle)
            normed_ref[slot] = (scaled * gains_ref[1:2] + biases_ref[4:5]).astype(jnp.bfloat16)
            final_ref[slot] = middle + biases_ref[5:6]
            return carry

        lax.fori_loop(0, slots, first, 0)

    def rows(slot, carry):
        pre = dot(normed_ref[slot], w_fc1_ref[...], MATMUL_NT) + fc1_bias_ref[0]
        below = 0.5 * (1.0 + lax.erf(pre * 0.5**0.5))
        hidden = (pre * below).astype(jnp.bfloat16)
        bell = jnp.exp(-0.5 * (pre * pre)) * (2.0 * math.pi) ** -0.5
        slope_ref[slot] = (below + pre * bell).astype(jnp.bfloat16)
        hidden_ref[slot] = hidden
        final_ref[slot] += dot(hidden, w_fc2_ref[0], MATMUL_NT)
        return carry

    lax.fori_loop(0, slots, rows, 0)


def mlp_forward(middle, w_fc1, w_fc2, gains, biases, fc1_bias):
    slots, padded, width = middle.shape
    blocks = w_fc2.shape[0]
    wide = (slots, padded, blocks * width)
    outs = [
        jax.ShapeDtypeStruct(middle.shape, jnp.bfloat16),
        jax.ShapeDtypeStruct(wide, jnp.bfloat16),
        jax.ShapeDtypeStruct(wide, jnp.bfloat16),
        jax.ShapeDtypeStruct(middle.shape, jnp.float32),
    ]
    wide_spec = pl.BlockSpec((slots, padded, width), lambda i: (0, 0, i))
    return pl.pallas_call(
        mlp_forward_kernel,
        grid=(blocks,),
        in_specs=[
            whole(middle.shape),
            pl.BlockSpec((width, width), lambda i: (i, 0)),
            pl.BlockSpec((1, width, width), lambda i: (i, 0, 0)),
            whole(gains.shape),
            whole(biases.shape),
            pl.BlockSpec((1, 1, width), lambda i: (i, 0, 0)),
        ],
        out_specs=[whole(middle.shape), wide_spec, wide_spec, whole(middle.shape)],
        out_shape=outs,
        compiler_params=params(),
        cost_estimate=worth(1),
        name="mlp_forward",
    )(middle, w_fc1, w_fc2, gains, biases, fc1_bias)


def mlp_backward_kernel(mode, cut, me_ref, grad_ref, middle_ref, normed_ref, hidden_ref, slope_ref, w_fc1_ref,
                        w_fc2_ref, gains_ref, *refs):
    share_count = 1 if mode == "joined" else 2
    share_refs = refs[:share_count]
    fc1_sums_ref, sums_ref, out_ref, branch_ref, pre_ref, total_ref, before_ref = refs[share_count:]
    block = pl.program_id(0)
    slots, padded, width = grad_ref.shape

    @pl.when(block == 0)
    def _():
        sums_ref[...] = jnp.zeros_like(sums_ref)

        def first(slot, carry):
            branch = grad_ref[slot].astype(jnp.bfloat16)
            branch_ref[pl.ds(pl.multiple_of(slot * padded, TILE_ROWS), padded), :] = branch
            sums_ref[2:3] += column_sums(branch)
            return carry

        lax.fori_loop(0, slots, first, 0)

    fc1_sums_ref[...] = jnp.zeros_like(fc1_sums_ref)

    def rows(slot, carry):
        here = pl.ds(pl.multiple_of(slot * padded, TILE_ROWS), padded)
        grad_hidden = dot(branch_ref[here, :], w_fc2_ref[0], MATMUL_NN)
        grad_pre = (grad_hidden * slope_ref[slot].astype(jnp.float32)).astype(jnp.bfloat16)
        pre_ref[here, :] = grad_pre
        fc1_sums_ref[0, 0:1] += column_sums(grad_pre)
        part = dot(grad_pre, w_fc1_ref[...], MATMUL_NN)

        @pl.when(block == 0)
        def _():
            total_ref[slot] = part

        @pl.when(block != 0)
        def _():
            total_ref[slot] += part

        return carry

    lax.fori_loop(0, slots, rows, 0)
    hidden = hidden_ref[...].reshape(slots * padded, width)
    normed = normed_ref[...].reshape(slots * padded, width)
    if mode == "plain":
        grad_fc1_ref, grad_fc2_ref = share_refs
        step = 2 * LANES
        for at in range(0, width, step):
            grad_fc2_ref[0, at : at + step, :] = dot(
                branch_ref[:, at : at + step], hidden, MATMUL_TN
            ).astype(jnp.bfloat16)
            grad_fc1_ref[at : at + step, :] = dot(
                pre_ref[:, at : at + step], normed, MATMUL_TN
            ).astype(jnp.bfloat16)
    else:
        tall = 4 * cut
        for at in range(0, width, SHARE_STEP):
            value = dot(pre_ref[:, at : at + SHARE_STEP], normed, MATMUL_TN)
            value = value.reshape(SHARE_STEP // tall, tall, width)
            for s in range(0, SHARE_STEP // tall, 2):
                pair = block * (width // tall // 2) + at // tall // 2 + s // 2
                put(share_refs, me_ref, pair, slice(0, tall), value[s], value[s + 1])
            value = dot(branch_ref[:, at : at + SHARE_STEP], hidden, MATMUL_TN)

            @pl.when(block % 2 == 0)
            def _():
                before_ref[at : at + SHARE_STEP, :] = value

            for odd in range(1, 4, 2):

                @pl.when(block == odd)
                def _():
                    before = before_ref[at : at + SHARE_STEP, :].reshape(-1, cut, width)
                    both = jnp.concatenate([before, value.reshape(-1, cut, width)], 1)
                    rows = slice(tall + (odd - 1) * cut, tall + (odd + 1) * cut)
                    for s in range(0, SHARE_STEP // cut, 2):
                        pair = at // cut // 2 + s // 2
                        put(share_refs, me_ref, pair, rows, both[s], both[s + 1])

    @pl.when(block == pl.num_programs(0) - 1)
    def _():
        def last(slot, carry):
            grad_normed = total_ref[slot]
            scaled, inv_std = norm_parts(middle_ref[slot])
            sums_ref[0:1] += column_sums(grad_normed * scaled)
            sums_ref[1:2] += column_sums(grad_normed)
            out_ref[slot] = grad_ref[slot] + norm_back(
                grad_normed, scaled, inv_std, gains_ref[1:2]
            )
            return carry

        lax.fori_loop(0, slots, last, 0)


def mlp_backward(mode, devices, me, grad, middle, normed, hidden, slope, w_fc1, w_fc2, gains):
    slots, padded, width = grad.shape
    blocks = w_fc2.shape[0]
    cut = width // devices
    fc1_spec = pl.BlockSpec((width, width), lambda i: (i, 0))
    fc2_spec = pl.BlockSpec((1, width, width), lambda i: (i, 0, 0))
    if mode == "plain":
        shares = [jax.ShapeDtypeStruct(v.shape, jnp.bfloat16) for v in (w_fc1, w_fc2)]
        share_specs = [fc1_spec, fc2_spec]
    else:
        shares = share_shapes(mode, devices, 8 * cut, width)
        share_specs = [whole(v.shape) for v in shares]
    outs = shares + [
        jax.ShapeDtypeStruct((blocks, 8, width), jnp.float32),
        jax.ShapeDtypeStruct((8, width), jnp.float32),
        jax.ShapeDtypeStruct(grad.shape, jnp.float32),
    ]
    wide_spec = pl.BlockSpec((slots, padded, width), lambda i: (0, 0, i))
    return pl.pallas_call(
        partial(mlp_backward_kernel, mode, cut),
        grid=(blocks,),
        in_specs=[pl.BlockSpec(memory_space=pltpu.SMEM)]
        + [whole(grad.shape), whole(grad.shape), whole(grad.shape)]
        + [wide_spec, wide_spec, fc1_spec, fc2_spec, whole(gains.shape)],
        out_specs=share_specs
        + [
            pl.BlockSpec((1, 8, width), lambda i: (i, 0, 0)),
            whole((8, width)),
            whole(grad.shape),
        ],
        out_shape=outs,
        scratch_shapes=[
            pltpu.VMEM((slots * padded, width), jnp.bfloat16),
            pltpu.VMEM((slots * padded, width), jnp.bfloat16),
            pltpu.VMEM(grad.shape, jnp.float32),
            pltpu.VMEM((width, width), jnp.float32),
        ],
        compiler_params=params(),
        cost_estimate=worth(BACKWARD_WORTH),
        name="mlp_backward",
    )(me, grad, middle, normed, hidden, slope, w_fc1, w_fc2, gains)


def attn_backward_kernel(mode, cut, me_ref, grad_ref, x_ref, normed_ref, mixed_ref, probs_ref, attended_ref,
                         w_qkv_ref, w_proj_ref, gains_ref, *refs):
    share_count = 1 if mode == "joined" else 2
    share_refs = refs[:share_count]
    sums_ref, out_ref, mixed_all, normed_all, attended_all, branch_all = refs[share_count:]
    slot = pl.program_id(0)
    _, padded, width = grad_ref.shape
    here = pl.ds(pl.multiple_of(slot * padded, TILE_ROWS), padded)

    @pl.when(slot == 0)
    def _():
        sums_ref[...] = jnp.zeros_like(sums_ref)

    branch = grad_ref[0].astype(jnp.bfloat16)
    branch_all[here, :] = branch
    normed_all[here, :] = normed_ref[0]
    attended_all[here, :] = attended_ref[0]
    grad_attended = dot(branch, w_proj_ref[...], MATMUL_NN).astype(jnp.bfloat16)
    for pair in range(width // LANES):
        at = pair * LANES
        query = mixed_ref[0, :, at : at + LANES]
        key = mixed_ref[0, :, width + at : width + at + LANES]
        value = mixed_ref[0, :, 2 * width + at : 2 * width + at + LANES]
        grad_pair = grad_attended[:, at : at + LANES]
        grad_query = grad_key = grad_value = 0.0
        for side in range(2):
            probs = probs_ref[0, 2 * pair + side]
            wide_probs = probs.astype(jnp.float32)
            grad_side = side_of(grad_pair, side)
            grad_value += dot(probs, grad_side, MATMUL_TN)
            grad_probs = dot(grad_side, value, MATMUL_NT)
            row_inner = jnp.sum(grad_probs * wide_probs, -1, keepdims=True)
            grad_scores = (wide_probs * (grad_probs - row_inner)).astype(jnp.bfloat16)
            grad_query += dot(grad_scores, side_of(key, side), MATMUL_NN)
            grad_key += dot(grad_scores, side_of(query, side), MATMUL_TN)
        grad_query = (grad_query * HEAD_DIM ** (-0.5)).astype(jnp.bfloat16)
        mixed_all[here, at : at + LANES] = grad_query
        mixed_all[here, width + at : width + at + LANES] = grad_key.astype(jnp.bfloat16)
        mixed_all[here, 2 * width + at : 2 * width + at + LANES] = grad_value.astype(jnp.bfloat16)
    grad_mixed = mixed_all[here, :]
    sums_ref[2:3] += column_sums(grad_mixed[:, :width])
    sums_ref[3:4] += column_sums(grad_mixed[:, 2 * width :])
    sums_ref[4:5] += column_sums(branch)
    grad_normed = dot(grad_mixed, w_qkv_ref[...], MATMUL_NN)
    scaled, inv_std = norm_parts(x_ref[0])
    sums_ref[0:1] += column_sums(grad_normed * scaled)
    sums_ref[1:2] += column_sums(grad_normed)
    out_ref[0] = grad_ref[0] + norm_back(grad_normed, scaled, inv_std, gains_ref[0:1])

    @pl.when(slot == pl.num_programs(0) - 1)
    def _():
        if mode == "plain":
            grad_qkv_ref, grad_proj_ref = share_refs
            step = 2 * LANES
            for at in range(0, 3 * width, step):
                grad_qkv_ref[at : at + step, :] = dot(
                    mixed_all[:, at : at + step], normed_all[...], MATMUL_TN
                ).astype(jnp.bfloat16)
            for at in range(0, width, step):
                grad_proj_ref[at : at + step, :] = dot(
                    branch_all[:, at : at + step], attended_all[...], MATMUL_TN
                ).astype(jnp.bfloat16)
        else:
            for at in range(0, width, SHARE_STEP):
                three = slice(3 * at, 3 * (at + SHARE_STEP))
                value = dot(mixed_all[:, three], normed_all[...], MATMUL_TN)
                more = dot(
                    branch_all[:, at : at + SHARE_STEP], attended_all[...], MATMUL_TN
                )
                both = jnp.concatenate(
                    [value.reshape(-1, 3 * cut, width), more.reshape(-1, cut, width)], 1
                )
                for s in range(0, SHARE_STEP // cut, 2):
                    pair = at // cut // 2 + s // 2
                    put(share_refs, me_ref, pair, slice(0, 4 * cut), both[s], both[s + 1])


def attn_backward(mode, devices, me, grad, state, normed, mixed, probs, attended, w_qkv, w_proj, gains, length):
    slots, padded, width = grad.shape
    cut = width // devices
    if mode == "plain":
        shares = [jax.ShapeDtypeStruct(v.shape, jnp.bfloat16) for v in (w_qkv, w_proj)]
    else:
        shares = share_shapes(mode, devices, 4 * cut + TILE_ROWS, width)
    outs = shares + [
        jax.ShapeDtypeStruct((8, width), jnp.float32),
        jax.ShapeDtypeStruct(grad.shape, jnp.float32),
    ]
    sliced = (grad, state, normed, mixed, probs, attended)
    return pl.pallas_call(
        partial(attn_backward_kernel, mode, cut),
        grid=(slots,),
        in_specs=[pl.BlockSpec(memory_space=pltpu.SMEM)]
        + [slot_block(v.shape) for v in sliced]
        + [whole(v.shape) for v in (w_qkv, w_proj, gains)],
        out_specs=[whole(o.shape) for o in outs[:-1]] + [slot_block(grad.shape)],
        out_shape=outs,
        scratch_shapes=[
            pltpu.VMEM((slots * padded, 3 * width), jnp.bfloat16),
            pltpu.VMEM((slots * padded, width), jnp.bfloat16),
            pltpu.VMEM((slots * padded, width), jnp.bfloat16),
            pltpu.VMEM((slots * padded, width), jnp.bfloat16),
        ],
        compiler_params=params(),
        cost_estimate=worth(length),
        name="attn_backward",
    )(me, *sliced, w_qkv, w_proj, gains)


def spread(share, place, refs):
    at = 0
    for ref in refs:
        rows = ref.shape[-2]
        for block in range(ref.shape[0]) if len(ref.shape) == 4 else [None]:
            piece = share[at : at + rows].astype(jnp.bfloat16)
            at += rows
            if block is None:
                ref[place] = piece
            else:
                ref[block, place] = piece


def unpack_kernel(blob_ref, *refs):
    for i in range(blob_ref.shape[0]):
        spread(blob_ref[i].astype(jnp.float32), i, refs)


def unpack_relative_kernel(count, me_ref, *refs):
    chips = pl.num_programs(0)
    for i in range(count):
        place = 2 * chips * (i // 2) + 2 * pl.program_id(0) + i % 2
        spread(refs[i][0].astype(jnp.float32), place ^ me_ref[0], refs[count:])


def unpack_whole(blob, shapes):
    devices, rows, width = blob.shape
    step = 4
    specs = [
        pl.BlockSpec((step, *s[1:]), lambda i: (i, 0, 0))
        if len(s) == 3
        else pl.BlockSpec((s[0], step, *s[2:]), lambda i: (0, i, 0, 0))
        for s in shapes
    ]
    return pl.pallas_call(
        unpack_kernel,
        grid=(devices // step,),
        in_specs=[pl.BlockSpec((step, rows, width), lambda i: (i, 0, 0))],
        out_specs=specs,
        out_shape=[jax.ShapeDtypeStruct(s, jnp.bfloat16) for s in shapes],
        compiler_params=params(),
        cost_estimate=worth(1),
        name="unpack_whole",
    )(blob)


def unpack_relative(pieces, me, shapes):
    return pl.pallas_call(
        partial(unpack_relative_kernel, len(pieces)),
        grid=(pieces[0].shape[0],),
        in_specs=[pl.BlockSpec(memory_space=pltpu.SMEM)] + [slot_block(p.shape) for p in pieces],
        out_specs=[whole(s) for s in shapes],
        out_shape=[jax.ShapeDtypeStruct(s, jnp.bfloat16) for s in shapes],
        compiler_params=params(),
        cost_estimate=worth(1),
        name="unpack_relative",
    )(me, *pieces)


AXES = ("dp", "fsdp")


def pack_layer(w_qkv, w_proj, w_fc1, w_fc2, gains, biases, fc1_bias):
    width, tall = w_qkv.shape[0], w_fc2.shape[0]
    cut = w_fc2.T.reshape(w_fc2.shape[1], tall // width, width).transpose(1, 0, 2)
    small = jnp.concatenate([gains.reshape(-1), biases.reshape(-1), fc1_bias.reshape(-1)])
    small = jnp.pad(small, (0, -small.size % width)).reshape(-1, width)
    small = jnp.pad(small, ((0, -small.shape[0] % 16), (0, 0)))
    return jnp.concatenate([w_qkv.T, w_proj.T, w_fc1.T, cut.reshape(-1, width), small], 0)


def unpack_layer(blob, shapes):
    devices, _, width = blob.shape
    qkv, proj, fc1, fc2, gains, biases, fc1_bias = shapes
    at = 0
    parts = []
    for columns in (qkv[1], proj[1], fc1[1]):
        parts.append(blob[:, at : at + columns].reshape(-1, width))
        at += columns
    blocks = fc2[0] // width
    cut = blob[:, at : at + blocks * fc2[1]].reshape(devices, blocks, fc2[1], width)
    parts.append(cut.transpose(1, 0, 2, 3).reshape(blocks, devices * fc2[1], width))
    at += blocks * fc2[1]
    small = unpack_small(blob[:, at:], (gains, biases, fc1_bias))
    small[2] = small[2].reshape(blocks, 1, width)
    return tuple(parts) + tuple(small)


def unpack_small(small, shapes):
    devices = small.shape[0]
    small = small.reshape(devices, -1)
    parts, start = [], 0
    for rows, columns in shapes:
        piece = small[:, start : start + rows * columns].reshape(devices, rows, columns)
        piece = piece.transpose(1, 0, 2).astype(jnp.float32)
        parts.append(piece.reshape(rows, devices * columns))
        start += rows * columns
    return parts


def pack_grads(grads, shapes, total_rows, devices):
    grad_qkv, grad_proj, grad_fc1, grad_fc2, gains_grad, biases_grad, fc1_grad = grads
    width = grad_qkv.shape[1]
    qkv, proj, fc1, fc2, gains, biases, fc1_bias = shapes
    blob = jnp.zeros((devices, total_rows, width), jnp.bfloat16)
    at = 0
    for value in (grad_qkv, grad_proj, grad_fc1):
        rows = value.shape[0] // devices
        blob = blob.at[:, at : at + rows].set(
            value.astype(jnp.bfloat16).reshape(devices, rows, width)
        )
        at += rows
    blocks = fc2[0] // width
    cut = grad_fc2.reshape(blocks, devices, fc2[1], width).transpose(1, 0, 2, 3)
    blob = blob.at[:, at : at + blocks * fc2[1]].set(cut.reshape(devices, -1, width))
    at += blocks * fc2[1]
    small = []
    for value, (rows, columns) in ((gains_grad, gains), (biases_grad, biases), (fc1_grad, fc1_bias)):
        small.append(value.reshape(rows, devices, columns).transpose(1, 0, 2).reshape(devices, -1))
    small = jnp.concatenate(small, 1).astype(jnp.bfloat16)
    small = jnp.pad(small, ((0, 0), (0, -small.shape[1] % width))).reshape(devices, -1, width)
    return blob.at[:, at : at + small.shape[1]].set(small)


def unpack_grads(blob, shapes):
    width = blob.shape[1]
    qkv, proj, fc1, fc2, gains, biases, fc1_bias = shapes
    blob = blob.astype(jnp.float32)
    at = 0
    parts = []
    for columns in (qkv[1], proj[1], fc1[1]):
        parts.append(blob[at : at + columns].T)
        at += columns
    blocks = fc2[0] // width
    cut = blob[at : at + blocks * fc2[1]].reshape(blocks, fc2[1], width)
    parts.append(cut.transpose(0, 2, 1).reshape(fc2))
    at += blocks * fc2[1]
    small = blob[at:].reshape(-1)
    start = 0
    for rows, columns in (gains, biases, fc1_bias):
        parts.append(small[start : start + rows * columns].reshape(rows, columns))
        start += rows * columns
    return tuple(parts)


def small_shares(values, devices):
    cut = [v.reshape(v.shape[0], devices, -1).transpose(1, 0, 2) for v in values]
    return jnp.concatenate([v.reshape(devices, -1) for v in cut], 1).astype(jnp.bfloat16)


def small_rows(row, width):
    row = jnp.pad(row, ((0, 0), (0, -row.shape[1] % (TILE_ROWS * width))))
    return row.reshape(row.shape[0], -1, width)


def swap(value, axis, mask, size):
    return lax.ppermute(value, axis, [(i, i ^ mask) for i in range(size)])


def total_of(values):
    return sum(v.astype(jnp.float32) for v in values).astype(jnp.bfloat16)


class Exchange:
    def __init__(self, mine, other, fsdp_size, orders):
        rows, width = mine.shape[-2:]
        self.fsdp_size = fsdp_size
        self.orders = [list(order) for order in orders]
        self.kept = mine
        self.shape = (2, 2, fsdp_size // 2, rows // len(orders), width)
        self.pending = None if other is None else [[swap(other, "fsdp", 1, fsdp_size)]]

    def sums(self):
        if self.pending is None:
            return [self.kept]
        if isinstance(self.kept, list):
            return [total_of([k, *got]) for k, got in zip(self.kept, self.pending)]
        got = self.pending[0][0]
        rows = self.shape[3]
        cuts = [slice(i * rows, (i + 1) * rows) for i in range(len(self.orders))]
        return [total_of([self.kept[:, c], got[:, c]]).reshape(self.shape) for c in cuts]

    def step(self):
        kept, pending = [], []
        for value, order in zip(self.sums(), self.orders):
            stage = order.pop(0)
            if stage == "z":
                kept.append(value[:, :, :1])
                pending.append(
                    [
                        swap(value[:, :, i : i + 1], "fsdp", 2 * i, self.fsdp_size)
                        for i in range(1, self.fsdp_size // 2)
                    ]
                )
            elif stage == "x":
                kept.append(value[:, :1])
                pending.append([swap(value[:, 1:], "dp", 1, 4)])
            elif stage == "y":
                kept.append(value[:1])
                pending.append([swap(value[1:], "dp", 2, 4)])
            else:
                kept.append(value[:1, :1])
                pending.append(
                    [
                        swap(value[i // 2 : i // 2 + 1, i % 2 : i % 2 + 1], "dp", i, 4)
                        for i in range(1, 4)
                    ]
                )
        self.kept, self.pending = kept, pending

    def result(self):
        return jnp.concatenate([v.reshape(self.shape[3:]) for v in self.sums()], 0)


def gate(values, *exchanges):
    values, arrived = lax.optimization_barrier((values, [e.pending for e in exchanges]))
    for exchange, pending in zip(exchanges, arrived):
        exchange.pending = pending
    return values


HALVES = (("x", "y"), ("y", "x"))
WHOLE = (("xy", "z"),)


def on_device(dp_size, fsdp_size, images, counts, cotangent, *weights):
    slots, seq_len, width = images.shape
    layer_count = weights[0].shape[0]
    shapes = [w.shape[1:] for w in weights]
    devices = dp_size * fsdp_size
    cut = width // devices
    direct = dp_size == 4 and layer_count == 2 and cut % 8 == 0 and SHARE_STEP % (8 * cut) == 0 and devices * cut == width
    live = (jnp.arange(slots) < counts[0]).astype(jnp.float32)[:, None, None]
    me = lax.axis_index("dp") * fsdp_size + lax.axis_index("fsdp")
    place = jnp.arange(devices)
    place = (jnp.bitwise_xor(2 * (place % (devices // 2)) + place // (devices // 2), me))[:, None]
    relative = (place == jnp.arange(devices)[None]).astype(jnp.bfloat16)
    me = me.astype(jnp.int32).reshape(1)
    extra = ((0, 0), (0, -seq_len % TILE_ROWS), (0, 0))
    state = jnp.pad(images.astype(jnp.float32), extra)
    blocks = shapes[3][0] // width
    every = [(layer_count * n, m) for n, m in shapes[4:]]
    share_rows = -(-sum(n * m for n, m in every) // width)
    share_rows = -(-share_rows // TILE_ROWS) * TILE_ROWS
    ahead = [(devices, 3 * cut, width), (devices, cut, width)]
    behind = [(devices, 4 * cut, width), (blocks, devices, cut, width)]
    little = [(devices, share_rows, width)]

    def attn_of(layer_index, state):
        w_qkv, w_proj, _, _, gains, biases, _ = gathered[layer_index]
        return (state, *attn_forward(state, w_qkv, w_proj, gains, biases, seq_len))

    def mlp_of(layer_index, middle):
        _, _, w_fc1, w_fc2, gains, biases, fc1_bias = gathered[layer_index]
        return mlp_forward(middle, w_fc1, w_fc2, gains, biases, fc1_bias)

    shares = [pack_layer(*(w[i] for w in weights)) for i in range(layer_count)]
    share = shares[0]
    grad_state = jnp.pad(cotangent.astype(jnp.float32) * live, extra)
    if direct:
        row = jnp.concatenate([w.reshape(1, -1) for w in weights[4:]], 1)
        row = jnp.pad(row, ((0, 0), (0, share_rows * width - row.shape[1])))
        share = jnp.concatenate([share[: 12 * cut], row.reshape(-1, width)], 0)
        blob = lax.all_gather(share, AXES, axis=0, tiled=False)
        late = shares[1][4 * cut : 12 * cut]
        blob_one = lax.all_gather(shares[1][: 4 * cut], AXES, axis=0, tiled=False)
        blob, late = lax.optimization_barrier((blob, late))
        rows = [late] + [swap(late, "fsdp", 2 * i, fsdp_size) for i in range(1, fsdp_size // 2)]
        *parts, small = unpack_whole(blob, ahead + behind + little)
        parts = [v.reshape(-1, width) for v in parts[:3]] + [parts[3].reshape(blocks, -1, width)]
        little_all = unpack_small(small, every)
        little_of = [
            [v[i * n : (i + 1) * n] for v, (n, _) in zip(little_all, shapes[4:])]
            for i in range(layer_count)
        ]
        for i in range(layer_count):
            little_of[i][2] = little_of[i][2].reshape(blocks, 1, width)
        parts, little_of = lax.optimization_barrier((parts, little_of))
        gathered = [(*parts, *little_of[0]), None]
        *saved, middle = attn_of(0, state)
        middle, rows = lax.optimization_barrier((middle, rows))
        rows = jnp.stack(rows)
        near = [rows] + [swap(rows, "dp", i, dp_size) for i in range(1, dp_size)]
        *more, final = mlp_of(0, middle)
        kept = [(*saved, middle, *more)]
        blob_one, final, grad_state = lax.optimization_barrier((blob_one, final, grad_state))
        w_qkv, w_proj = unpack_whole(blob_one, ahead)
        w_qkv, near = lax.optimization_barrier((w_qkv, near))
        pieces = [v for n in near for v in (n, swap(n, "fsdp", 1, fsdp_size))]
        w_qkv, w_proj = w_qkv.reshape(-1, width), w_proj.reshape(-1, width)
        gathered[1] = (w_qkv, w_proj, None, None, *little_of[1])
        *saved, middle = attn_of(1, final)
        middle, pieces = lax.optimization_barrier((middle, pieces))
        w_fc1, w_fc2 = unpack_relative(pieces, me, behind)
        w_fc1, w_fc2 = w_fc1.reshape(-1, width), w_fc2.reshape(blocks, -1, width)
        gathered[1] = (w_qkv, w_proj, w_fc1, w_fc2, *gathered[1][4:])
        *more, state = mlp_of(1, middle)
        kept.append((*saved, middle, *more))
    else:
        gathered = [lax.all_gather(v, AXES, axis=0, tiled=False) for v in shares]
        kept = []
        for layer_index in range(layer_count):
            blob, state = lax.optimization_barrier((gathered[layer_index], state))
            gathered[layer_index] = unpack_layer(blob, shapes)
            *saved, middle = attn_of(layer_index, state)
            *more, state = mlp_of(layer_index, middle)
            kept.append((*saved, middle, *more))
    layer_grads = [None] * layer_count

    def small_of(mlp, attn):
        fc1_sums, mlp_sums = mlp
        gains_grad = jnp.stack([attn[0], mlp_sums[0]])
        biases_grad = jnp.stack([attn[1], attn[2], attn[3], attn[4], mlp_sums[1], mlp_sums[2]])
        return (gains_grad, biases_grad, fc1_sums[:, 0].reshape(1, -1))

    def mlp_part(layer_index, mode, grad_state):
        w_fc1, w_fc2, gains = gathered[layer_index][2:5]
        middle, normed, hidden, slope = kept[layer_index][5:]
        *shares, fc1_sums, sums, grad_middle = mlp_backward(
            mode, devices, me, grad_state, middle, normed, hidden, slope, w_fc1, w_fc2, gains
        )
        return shares, (fc1_sums, sums), grad_middle

    def attn_part(layer_index, mode, grad_middle):
        w_qkv, w_proj, gains = (gathered[layer_index][i] for i in (0, 1, 4))
        *shares, sums, grad_state = attn_backward(
            mode, devices, me, grad_middle, *kept[layer_index][:5], w_qkv, w_proj, gains,
            1 if layer_index else 200
        )
        return shares, sums, grad_state

    def with_small(shares, mlp, attn):
        row = small_shares(small_of(mlp, attn), devices)
        row = jnp.dot(relative, row, preferred_element_type=jnp.float32).astype(jnp.bfloat16)
        row = small_rows(row, width)
        count = shares[0].shape[0]
        return [v.at[:, 4 * cut :].set(row[i * count : (i + 1) * count]) for i, v in enumerate(shares)]

    def owned(attn_sum, mlp_sum):
        summed = jnp.concatenate([attn_sum[: 4 * cut], mlp_sum, attn_sum[4 * cut :]], 0)
        return unpack_grads(summed, shapes)

    if direct:
        shares, mlp, grad_middle = mlp_part(1, "split", grad_state)
        mlp_one = Exchange(*shares, fsdp_size, HALVES)
        shares, attn, grad_state = attn_part(1, "split", grad_middle)
        shares, attn, grad_state = gate((shares, attn, grad_state), mlp_one)
        mlp_one.step()
        attn_one = Exchange(*with_small(shares, mlp, attn), fsdp_size, WHOLE)
        shares, mlp, grad_middle = mlp_part(0, "joined", grad_state)
        mlp_zero = lax.psum_scatter(shares[0], AXES, scatter_dimension=0, tiled=False)
        grad_middle, mlp = gate((grad_middle, mlp), mlp_one, attn_one)
        mlp_one.step()
        attn_one.step()
        shares, attn, grad_state = attn_part(0, "split", grad_middle)
        shares, attn, grad_state = gate((shares, attn, grad_state), mlp_one, attn_one)
        late = mlp_one.sums() + attn_one.sums()
        late = Exchange(jnp.concatenate(late, 3), None, fsdp_size, (("z",),))
        late.step()
        attn, state = lax.optimization_barrier((attn, state))
        attn_zero = Exchange(*with_small(shares, mlp, attn), fsdp_size, WHOLE)
        attn_zero.step()
        arrived = attn_zero.pending
        late.pending, arrived = lax.optimization_barrier((late.pending, arrived))
        attn_zero.step()
        late = late.result()
        layer_grads[1] = owned(late[8 * cut :], late[: 8 * cut])
        layer_grads[0] = owned(attn_zero.result(), mlp_zero)
    else:
        for layer_index in reversed(range(layer_count)):
            mlp_shares, mlp, grad_middle = mlp_part(layer_index, "plain", grad_state)
            attn_shares, attn, grad_state = attn_part(layer_index, "plain", grad_middle)
            grads = (*attn_shares, *mlp_shares, *small_of(mlp, attn))
            packed = pack_grads(grads, shapes, share.shape[0], devices)
            summed = lax.psum_scatter(packed, AXES, scatter_dimension=0, tiled=False)
            layer_grads[layer_index] = unpack_grads(summed, shapes)
    block_output = (state[:, :seq_len] * live).astype(jnp.bfloat16)
    stacked = tuple((jnp.stack([entry[member] for entry in layer_grads]) for member in range(7)))
    return (block_output, grad_state[:, :seq_len], *stacked)


def solution(mesh):
    placed = (
        P(("dp", "fsdp"), None, None),
        P(("dp", "fsdp")),
        P(("dp", "fsdp"), None, None),
        P(None, None, ("dp", "fsdp")),
        P(None, None, ("dp", "fsdp")),
        P(None, None, ("dp", "fsdp")),
        P(None, None, ("dp", "fsdp")),
        P(None, None, ("dp", "fsdp")),
        P(None, None, ("dp", "fsdp")),
        P(None, None, ("dp", "fsdp")),
    )
    return jax.shard_map(
        partial(on_device, mesh.shape["dp"], mesh.shape["fsdp"]),
        mesh=mesh,
        in_specs=placed,
        out_specs=(
            P(("dp", "fsdp"), None, None),
            P(("dp", "fsdp"), None, None),
            P(None, None, ("dp", "fsdp")),
            P(None, None, ("dp", "fsdp")),
            P(None, None, ("dp", "fsdp")),
            P(None, None, ("dp", "fsdp")),
            P(None, None, ("dp", "fsdp")),
            P(None, None, ("dp", "fsdp")),
            P(None, None, ("dp", "fsdp")),
        ),
        check_vma=False,
    )
```
